128 devices in a mesh: dp: 16 (over z, y_lo, core), tensor: 8 (over x, y_hi).
Axes of the slice: x: 4, y: 4 (y_hi: 2, y_lo: 2; y = y_hi * 2 + y_lo), z: 4, core: 2. Of those that a mesh axis runs over, the one named last changes fastest.
Arguments:
- activations: bfloat16 [24576, 14336], P('dp', 'tensor'), as said below
- out_grads: bfloat16 [24576, 4096], P('dp', 'tensor'), as said below
- noise: float32 [4096, 14336], P('dp', 'tensor'), may hold values from -96 to 96
Outputs:
- noisy_grad: float32 [4096, 14336], P('dp', 'tensor')
The draws below stay inside these ranges and needn't reach their ends.
Inputs may be any that keep to these rules, and one draw needn't show every extreme that they name: `activations`: Finite; each row is one token's hidden units. `out_grads`: Finite; each row is one token's output gradient.
All inputs are finite; a program needn't handle non-finite values.
Results may differ from the reference program's by a relative error of at most 0.0003.
Values may be sent and summed in bfloat16 or wider, within the bound.
A program may use at most 128 MiB of HBM per device.

```python
import jax
import jax.numpy as jnp
from jax import lax

D = 4096
FF = 14336
SEQ = 256
TOKENS = 24576


def draw_activations(key, part):
    key = jax.random.fold_in(key, 11)
    keys = jax.random.split(key, 3)
    rising = jnp.sqrt(3.0) ** (jnp.arange(FF, dtype=jnp.float32) / FF)
    column = rising * jnp.exp(jax.random.uniform(keys[1], (FF,), jnp.float32, jnp.log(0.5), jnp.log(2.0)))
    row = jnp.exp(jax.random.uniform(keys[2], (TOKENS, 1), jnp.float32, jnp.log(0.3), jnp.log(3.0)))
    base = jax.random.normal(keys[0], (TOKENS, FF), jnp.float32)
    return (base * row * column).astype(jnp.bfloat16)


def draw_out_grads(key, part):
    key = jax.random.fold_in(key, 12)
    keys = jax.random.split(key, 4)
    rising = jnp.sqrt(3.0) ** (jnp.arange(D, dtype=jnp.float32) / D)
    column = rising * jnp.exp(jax.random.uniform(keys[1], (D,), jnp.float32, jnp.log(0.5), jnp.log(2.0)))
    row = jnp.exp(jax.random.uniform(keys[2], (TOKENS, 1), jnp.float32, jnp.log(0.3), jnp.log(3.0)))
    example = jnp.exp(jax.random.uniform(keys[3], (TOKENS // SEQ,), jnp.float32, jnp.log(0.01), jnp.log(0.1)))
    example = jnp.repeat(example, SEQ)[:, None]
    base = jax.random.normal(keys[0], (TOKENS, D), jnp.float32)
    return (base * row * column * example).astype(jnp.bfloat16)


def block_scale(stream_key, dims, cuts, least, high):
    loudness = 1.0
    for position, shards_of in cuts:
        steps = jax.random.uniform(jax.random.fold_in(jax.random.fold_in(stream_key, 6), position), (shards_of,), jnp.float32, least / len(cuts), high / len(cuts))
        loudness = loudness * jnp.repeat(jnp.exp(steps), dims[position] // shards_of).reshape((-1,) + (1,) * (len(dims) - 1 - position))
    return loudness


def centred(rng, dims, deviation, most, cuts=(), kind=jnp.bfloat16):
    result = deviation * jax.random.normal(rng, dims, jnp.float32)
    if cuts:
        result = result * block_scale(rng, dims, cuts, -0.22, 0.18)
    return jnp.clip(result, -most, most).astype(kind)


def setup_inputs(seed: int = 0) -> dict:
    streams_of = jax.random.split(jax.random.key(seed), 4)
    return {
        "activations": draw_activations(jax.random.fold_in(streams_of[3], 71), 0),
        "out_grads": draw_out_grads(jax.random.fold_in(streams_of[3], 71), 0),
        "noise": centred(streams_of[2], (D, FF), 16.0, 96.0, ((0, 16), (1, 8)), jnp.float32),
    }


def reference(activations, out_grads, noise):
    count = TOKENS // SEQ
    acts = activations.reshape(count, SEQ, FF).astype(jnp.float32)
    grads = out_grads.reshape(count, SEQ, D).astype(jnp.float32)

    def one_norm(pair):
        act_rows, grad_rows = pair
        act_gram = jnp.einsum('sf,tf->st', act_rows, act_rows)
        grad_gram = jnp.einsum('sd,td->st', grad_rows, grad_rows)
        return jnp.sum(act_gram * grad_gram)
    sq_norm = lax.map(one_norm, (acts, grads))
    bound = 0.15 * jnp.sqrt(jnp.float32(SEQ) * FF * D)
    factor = jnp.minimum(1.0, bound / jnp.sqrt(sq_norm + 1e-06))
    act_blocks = activations.reshape(count, SEQ, FF)
    grad_blocks = out_grads.reshape(count, SEQ, D)

    def accumulate(total, items):
        act_rows, grad_rows, weight = items
        return (total + weight * jnp.dot(grad_rows.T, act_rows, preferred_element_type=jnp.float32), None)
    start = jnp.zeros((D, FF), jnp.float32)
    grad_sum, _ = lax.scan(accumulate, start, (act_blocks, grad_blocks, factor))
    return (grad_sum + noise) / count
```

```python
import functools

import jax
import jax.numpy as jnp
from jax import lax
from jax.experimental import pallas as pl
from jax.experimental.pallas import tpu as pltpu
from jax.sharding import PartitionSpec as P

MESH = pl.DeviceIdType.MESH
F32 = jnp.float32
BF16 = jnp.bfloat16
D = 4096
FF = 14336
SEQ = 256
EX = 6
TOK = EX * SEQ
FL = 1792
DL = 512
PH = 8
RW = 32
SLOTS = 4
GROWS = EX * 32 + 8
COUNT = 96
LANES = 128


def kernel(
    act, g, out,
    H, gin, gT, Gb, GS, GR, SQm, SQ, FAC, Pb, ZR, YR, OS,
    hsem, gsem, hx, gx, gl, gramS, gramR, sqS, sqR, facx, gsnd, grcv, gy, zsnd, zrcv, yrcv, osem,
):
    dp = lax.axis_index("dp")
    t = lax.axis_index("tensor")
    z, yl, c = dp // 4, (dp // 2) % 2, dp % 2
    x, yh = t // 2, t % 2
    oc = 1 - c
    sib = (z * 4 + yl * 2 + oc, t)
    xp, xm = (x + 1) % 4, (x + 3) % 4
    right = (dp, xp * 2 + yh)
    left = (dp, xm * 2 + yh)
    ypeer = (dp, x * 2 + 1 - yh)
    zp, zm, zo = (z + 1) % 4, (z + 3) % 4, (z + 2) % 4
    up = (zp * 4 + yl * 2 + c, t)
    down = (zm * 4 + yl * 2 + c, t)
    ylo = (z * 4 + (1 - yl) * 2 + c, t)

    def remote(src, dst, ssem, rsem, dev):
        return pltpu.make_async_remote_copy(
            src_ref=src, dst_ref=dst, send_sem=ssem, recv_sem=rsem, device_id=dev, device_id_type=MESH
        )

    g_in = pltpu.make_async_copy(g, gin, gsem)
    g_in.start()

    def h_in(e):
        rows = pl.ds(e * SEQ, SEQ)
        return pltpu.make_async_copy(act.at[rows], H.at[c, rows], hsem.at[e])

    for e in range(EX):
        h_in(e).start()

    barrier = pltpu.get_barrier_semaphore()
    partners = [(dp, (t + j) % 8) for j in range(1, 8)] + [sib, up, down, ylo]
    for dev in partners:
        pl.semaphore_signal(barrier, inc=1, device_id=dev, device_id_type=MESH)
    pl.semaphore_wait(barrier, len(partners))

    def shard_copy(k, owner, ssem, rsem, dev):
        return remote(Gb.at[k, owner], Gb.at[k, owner], ssem, rsem, dev)

    def own_y(k):
        return shard_copy(k, t, gsnd.at[k, 0], gy.at[k], ypeer)

    def own_x(k, d):
        return shard_copy(k, t, gsnd.at[k, 1 + d], grcv.at[k, d, 0], right if d == 0 else left)

    def peer_x(k, d):
        return shard_copy(k, x * 2 + 1 - yh, gsnd.at[k, 3 + d], grcv.at[k, d, 1], right if d == 0 else left)

    def fwd_x(k, d):
        owner = xm * 2 if d == 0 else xp * 2 + 1
        return shard_copy(k, owner, gsnd.at[k, 5 + d], grcv.at[k, d, 2], right if d == 0 else left)

    def wait_shard(k, d, kind):
        shard_copy(k, t, gsnd.at[k, 0], grcv.at[k, d, kind], ypeer).wait_recv()

    def start_own_x(k):
        own_x(k, 0).start()
        own_x(k, 1).start()

    def start_peer_x(k):
        own_y(k).wait_recv()
        peer_x(k, 0).start()
        peer_x(k, 1).start()

    def start_fwd_x(k):
        wait_shard(k, 0, yh)
        fwd_x(k, 0).start()
        wait_shard(k, 1, 1 - yh)
        fwd_x(k, 1).start()

    def wait_rest(k):
        wait_shard(k, 0, 1 - yh)
        wait_shard(k, 1, yh)
        wait_shard(k, 0, 2)
        wait_shard(k, 1, 2)

    g_in.wait()
    for e in range(EX):
        tr = gin[e * SEQ : (e + 1) * SEQ, :].T
        gT[:, :, :, e * SEQ : (e + 1) * SEQ] = tr.reshape(2, PH, RW, SEQ)
    g_local = pltpu.make_async_copy(gT.at[c], Gb.at[:, t, c], gl)
    g_sib = remote(gT.at[oc], Gb.at[:, t, c], gx.at[0], gx.at[1], sib)
    g_local.start()
    g_sib.start()
    for e in range(EX):
        h_in(e).wait()
    h_sib = remote(H.at[c], H.at[c], hx.at[0], hx.at[1], sib)
    h_sib.start()
    g_local.wait()
    g_sib.wait()
    for k in range(2):
        own_y(k).start()
    start_own_x(0)

    i0 = lax.broadcasted_iota(jnp.int32, (LANES, LANES), 0)
    i1 = lax.broadcasted_iota(jnp.int32, (LANES, LANES), 1)
    e8 = lax.broadcasted_iota(jnp.int32, (8, LANES), 0)
    nt = (((1,), (1,)), ((), ()))

    def gram(e, diags):
        rows = pl.ds(pl.multiple_of(e * SEQ, SEQ), SEQ)
        result = []
        for m in range(2):
            r = H[c, rows, :] if m == 0 else gin[rows, :]
            a = lax.dot_general(r, r, nt, preferred_element_type=F32)
            packed = jnp.where(i0 >= i1, a[:LANES, :LANES], a[LANES:, LANES:])
            below = a[LANES:, :LANES]
            for r8 in range(8):
                part = packed if r8 < 4 else below
                lo = (r8 % 4) * 32
                GS[r8, pl.ds(pl.multiple_of(m * GROWS + e * 32, 8), 32), :] = part[lo : lo + 32]
            diag = jnp.sum(jnp.where(i0 == i1, a[LANES:, LANES:], 0.0), axis=0, keepdims=True)
            result.append(jnp.where(e8 == e, diag, diags[m]))
        return tuple(result)

    zero8 = jnp.zeros((8, LANES), F32)
    diags = lax.fori_loop(0, EX, gram, (zero8, zero8))
    for m in range(2):
        for r8 in range(8):
            GS[r8, m * GROWS + EX * 32 : (m + 1) * GROWS, :] = diags[m]

    def gram_copy(j):
        peer = (t + j) % 8
        return remote(GS.at[peer], GR.at[t], gramS.at[j], gramR.at[j], (dp, peer))

    for j in range(1, 8):
        gram_copy(j).start()
    GR[t] = GS[t]
    start_peer_x(0)
    own_y(2).start()
    start_own_x(1)
    start_fwd_x(0)
    start_peer_x(1)
    for j in range(1, 8):
        gram_copy(j).wait_recv()

    total = GR[0]
    for s in range(1, 8):
        total = total + GR[s]
    prod = total[:GROWS] * total[GROWS:]
    r32 = lax.broadcasted_iota(jnp.int32, (32, LANES), 0)
    l32 = lax.broadcasted_iota(jnp.int32, (32, LANES), 1)
    weight = jnp.where(l32 == r32 + t * 32, 1.0, 2.0)
    l8 = lax.broadcasted_iota(jnp.int32, (8, LANES), 1)
    mine = jnp.where(l8 // 16 == t, prod[EX * 32 :], 0.0)
    for e in range(EX):
        part = jnp.sum(prod[e * 32 : (e + 1) * 32] * weight, axis=0, keepdims=True)
        mine = mine + jnp.where(e8 == e, part, 0.0)
    SQm[...] = mine
    SQ[t] = mine

    def sq_copy(j):
        peer = (t + j) % 8
        return remote(SQm, SQ.at[t], sqS.at[j], sqR.at[j], (dp, peer))

    for j in range(1, 8):
        sq_copy(j).start()
    for j in range(1, 8):
        sq_copy(j).wait_recv()
    sq = SQ[0]
    for s in range(1, 8):
        sq = sq + SQ[s]
    sq = jnp.sum(sq, axis=1, keepdims=True)
    bound = jnp.float32(0.15) * jnp.sqrt(jnp.float32(SEQ) * FF * D)
    factor = jnp.minimum(1.0, bound / jnp.sqrt(jnp.maximum(sq, 0.0) + 1e-06))
    FAC[c] = jnp.broadcast_to(factor, (8, 256))
    fac_sib = remote(FAC.at[c], FAC.at[c], facx.at[0], facx.at[1], sib)
    fac_sib.start()
    h_sib.wait()
    fac_sib.wait()
    for j in range(1, 8):
        gram_copy(j).wait_send()
        sq_copy(j).wait_send()

    def compute(k, s):
        def block(n, carry):
            cols = pl.ds(pl.multiple_of(n * 256, 256), 256)
            acc = None
            for e in range(2 * EX):
                cs, j = divmod(e, EX)
                lhs = Gb[k, :, cs, :, j * SEQ : (j + 1) * SEQ].reshape(8 * RW, SEQ)
                rhs = H[cs, j * SEQ : (j + 1) * SEQ, cols]
                d = jnp.dot(lhs, rhs, preferred_element_type=F32) * FAC[cs, j : j + 1, :]
                acc = d if acc is None else acc + d
            Pb[s, :, :, :, cols] = acc.reshape(4, 2, RW, 256)
            return carry

        lax.fori_loop(0, FL // 256, block, 0)

    def z_copy(k, d, kind):
        s = k % SLOTS
        if kind == 0:
            src = Pb.at[s, zo, d]
        elif kind == 1:
            src = Pb.at[s, zp, 1] if d == 0 else Pb.at[s, zm, 0]
        else:
            src = Pb.at[s, zp, 0] if d == 0 else Pb.at[s, zm, 1]
        return remote(src, ZR.at[k, d, kind], zsnd.at[s, 2 * kind + d], zrcv.at[k, d, kind], up if d == 0 else down)

    def y_copy(k):
        s = k % SLOTS
        return remote(Pb.at[s, z, 1 - yl], YR.at[k], zsnd.at[s, 6], yrcv.at[k], ylo)

    def out_copy(k):
        return pltpu.make_async_copy(OS.at[k], out.at[pl.ds(pl.multiple_of(k * RW, RW), RW)], osem.at[k])

    def send_first(k):
        for kind in range(2):
            for d in range(2):
                z_copy(k, d, kind).start()

    def relay(k):
        s = k % SLOTS
        for d in range(2):
            z_copy(k, d, 0).wait_recv()
            dest = (zp, 0) if d == 0 else (zm, 1)
            Pb[s, dest[0], dest[1]] = Pb[s, dest[0], dest[1]] + ZR[k, d, 0]
            z_copy(k, d, 2).start()

    def last(k):
        s = k % SLOTS
        for kind in (1, 2):
            for d in range(2):
                z_copy(k, d, kind).wait_recv()
        Pb[s, z, 0] = Pb[s, z, 0] + ZR[k, 0, 2] + ZR[k, 1, 1]
        Pb[s, z, 1] = Pb[s, z, 1] + ZR[k, 0, 1] + ZR[k, 1, 2]
        y_copy(k).start()

    def finish(k):
        s = k % SLOTS
        y_copy(k).wait_recv()
        OS[k] = Pb[s, z, yl] + YR[k]
        out_copy(k).start()

    def free(k):
        for kind in range(3):
            for d in range(2):
                z_copy(k, d, kind).wait_send()
        y_copy(k).wait_send()

    def step(k, carry):
        @pl.when(k < PH)
        def _():
            wait_rest(k)

            @pl.when(k >= SLOTS)
            def _():
                free(k - SLOTS)

            compute(k, k % SLOTS)
            send_first(k)

        @pl.when(k + 3 < PH)
        def _():
            own_y(k + 3).start()

        @pl.when(k + 2 < PH)
        def _():
            start_own_x(k + 2)

        @pl.when(k + 1 < PH)
        def _():
            start_fwd_x(k + 1)

        @pl.when(k + 2 < PH)
        def _():
            start_peer_x(k + 2)

        @pl.when((k >= 1) & (k < PH + 1))
        def _():
            relay(k - 1)

        @pl.when((k >= 2) & (k < PH + 2))
        def _():
            last(k - 2)

        @pl.when(k >= 3)
        def _():
            finish(k - 3)

        return carry

    lax.fori_loop(0, PH + 3, step, 0)

    def drain(k, carry):
        own_y(k).wait_send()
        for d in range(2):
            own_x(k, d).wait_send()
            peer_x(k, d).wait_send()
            fwd_x(k, d).wait_send()
        out_copy(k).wait()
        return carry

    lax.fori_loop(0, PH, drain, 0)
    lax.fori_loop(PH - SLOTS, PH, lambda k, carry: (free(k), carry)[1], 0)


def per_device(activations, out_grads, noise):
    dma = pltpu.SemaphoreType.DMA
    summed = pl.pallas_call(
        kernel,
        out_shape=jax.ShapeDtypeStruct((256, FL), F32),
        in_specs=[pl.BlockSpec(memory_space=pl.ANY)] * 2,
        out_specs=pl.BlockSpec(memory_space=pl.ANY),
        scratch_shapes=[
            pltpu.VMEM((2, TOK, FL), BF16),
            pltpu.VMEM((TOK, DL), BF16),
            pltpu.VMEM((2, PH, RW, TOK), BF16),
            pltpu.VMEM((PH, 8, 2, RW, TOK), BF16),
            pltpu.VMEM((8, 2 * GROWS, LANES), F32),
            pltpu.VMEM((8, 2 * GROWS, LANES), F32),
            pltpu.VMEM((8, LANES), F32),
            pltpu.VMEM((8, 8, LANES), F32),
            pltpu.VMEM((2, 8, 256), F32),
            pltpu.VMEM((SLOTS, 4, 2, RW, FL), F32),
            pltpu.VMEM((PH, 2, 3, RW, FL), F32),
            pltpu.VMEM((PH, RW, FL), F32),
            pltpu.VMEM((PH, RW, FL), F32),
            dma((EX,)),
            dma,
            dma((2,)),
            dma((2,)),
            dma,
            dma((8,)),
            dma((8,)),
            dma((8,)),
            dma((8,)),
            dma((2,)),
            dma((PH, 7)),
            dma((PH, 2, 3)),
            dma((PH,)),
            dma((SLOTS, 7)),
            dma((PH, 2, 3)),
            dma((PH,)),
            dma((PH,)),
        ],
        compiler_params=pltpu.CompilerParams(
            collective_id=0, has_side_effects=True, vmem_limit_bytes=62 << 20
        ),
        cost_estimate=pl.CostEstimate(flops=24 * 10**9, bytes_accessed=9 * 10**6, transcendentals=0),
    )(activations, out_grads)
    return (summed + noise) / COUNT


def solution(mesh):
    return jax.shard_map(
        per_device,
        mesh=mesh,
        in_specs=(P("dp", "tensor"), P("dp", "tensor"), P("dp", "tensor")),
        out_specs=P("dp", "tensor"),
        check_vma=False,
    )
```

```python
import functools

import jax
import jax.numpy as jnp
from jax import lax
from jax.experimental import pallas as pl
from jax.experimental.pallas import tpu as pltpu
from jax.sharding import PartitionSpec as P

MESH = pl.DeviceIdType.MESH
F32 = jnp.float32
BF16 = jnp.bfloat16
D = 4096
FF = 14336
SEQ = 256
EX = 6
TOK = EX * SEQ
FL = 1792
DL = 512
PH = 8
RW = 32
SLOTS = 4
ZB = 5
ZC = ZB * 256
GROWS = EX * 32 + 8
COUNT = 96
LANES = 128


def kernel(
    act, g, out,
    H, gin, gT, Gb, GSA, GSG, RA1, A2, RA2, RG1, G2, RG2, SQm, SQ, FAC, Pz, Py, ZR, YR, YZ, WR, OS,
    hsem, gsem, hx, gx, gl, gramS, gramR, sqS, sqR, facx, gsnd, grcv, gy, zsnd, zrcv, yrcv, wsnd, wrcv, y1rcv, osem,
):
    dp = lax.axis_index("dp")
    t = lax.axis_index("tensor")
    z, yl, c = dp // 4, (dp // 2) % 2, dp % 2
    x, yh = t // 2, t % 2
    oc = 1 - c
    sib = (z * 4 + yl * 2 + oc, t)
    xp, xm = (x + 1) % 4, (x + 3) % 4
    right = (dp, xp * 2 + yh)
    left = (dp, xm * 2 + yh)
    ypeer = (dp, x * 2 + 1 - yh)
    zp, zm, zo = (z + 1) % 4, (z + 3) % 4, (z + 2) % 4
    up = (zp * 4 + yl * 2 + c, t)
    down = (zm * 4 + yl * 2 + c, t)
    ylo = (z * 4 + (1 - yl) * 2 + c, t)

    def remote(src, dst, ssem, rsem, dev):
        return pltpu.make_async_remote_copy(
            src_ref=src, dst_ref=dst, send_sem=ssem, recv_sem=rsem, device_id=dev, device_id_type=MESH
        )

    g_in = pltpu.make_async_copy(g, gin, gsem)
    g_in.start()

    def h_in(e):
        rows = pl.ds(e * SEQ, SEQ)
        return pltpu.make_async_copy(act.at[rows], H.at[c, rows], hsem.at[e])

    for e in range(EX):
        h_in(e).start()

    barrier = pltpu.get_barrier_semaphore()
    partners = [(dp, (t + j) % 8) for j in range(1, 8)] + [sib, up, down, ylo]
    for dev in partners:
        pl.semaphore_signal(barrier, inc=1, device_id=dev, device_id_type=MESH)

    def shard_copy(k, owner, ssem, rsem, dev):
        return remote(Gb.at[k, owner], Gb.at[k, owner], ssem, rsem, dev)

    def own_y(k):
        return shard_copy(k, t, gsnd.at[k, 0], gy.at[k], ypeer)

    def own_x(k, d):
        return shard_copy(k, t, gsnd.at[k, 1 + d], grcv.at[k, d, 0], right if d == 0 else left)

    def peer_x(k, d):
        return shard_copy(k, x * 2 + 1 - yh, gsnd.at[k, 3 + d], grcv.at[k, d, 1], right if d == 0 else left)

    def fwd_x(k, d):
        owner = xm * 2 if d == 0 else xp * 2 + 1
        return shard_copy(k, owner, gsnd.at[k, 5 + d], grcv.at[k, d, 2], right if d == 0 else left)

    def wait_shard(k, d, kind):
        shard_copy(k, t, gsnd.at[k, 0], grcv.at[k, d, kind], ypeer).wait_recv()

    def start_own_x(k):
        own_x(k, 0).start()
        own_x(k, 1).start()

    def start_peer_x(k):
        own_y(k).wait_recv()
        peer_x(k, 0).start()
        peer_x(k, 1).start()

    def start_fwd_x(k):
        wait_shard(k, 0, yh)
        fwd_x(k, 0).start()
        wait_shard(k, 1, 1 - yh)
        fwd_x(k, 1).start()

    def wait_rest(k):
        wait_shard(k, 0, 1 - yh)
        wait_shard(k, 1, yh)
        wait_shard(k, 0, 2)
        wait_shard(k, 1, 2)

    i0 = lax.broadcasted_iota(jnp.int32, (LANES, LANES), 0)
    i1 = lax.broadcasted_iota(jnp.int32, (LANES, LANES), 1)
    e8 = lax.broadcasted_iota(jnp.int32, (8, LANES), 0)
    nt = (((1,), (1,)), ((), ()))
    zero8 = jnp.zeros((8, LANES), F32)

    def gram(rows_of, piece):
        def one(e, diags):
            r = rows_of(e, pl.ds(pl.multiple_of(e * SEQ, SEQ), SEQ))
            a = lax.dot_general(r, r, nt, preferred_element_type=F32)
            packed = jnp.where(i0 >= i1, a[:LANES, :LANES], a[LANES:, LANES:])
            below = a[LANES:, :LANES]
            for owner in range(8):
                part = packed if owner < 4 else below
                lo = (owner % 4) * 32
                piece(owner, pl.ds(pl.multiple_of(e * 32, 32), 32), part[lo : lo + 32])
            diag = jnp.sum(jnp.where(i0 == i1, a[LANES:, LANES:], 0.0), axis=0, keepdims=True)
            return jnp.where(e8 == e, diag, diags)

        diags = lax.fori_loop(0, EX, one, zero8)
        for owner in range(8):
            piece(owner, slice(EX * 32, GROWS), diags)

    def piece_a(owner, rows, value):
        GSA[owner // 2, owner % 2, rows, :] = value

    def piece_g(owner, rows, value):
        GSG[owner % 2, owner // 2, rows, :] = value

    def rows_h(e, rows):
        h_in(e).wait()
        return H[c, rows, :]

    g_in.wait()
    gram(lambda e, rows: gin[rows, :], piece_g)
    pl.semaphore_wait(barrier, len(partners))
    g_one = remote(GSG.at[1 - yh], RG1, gramS.at[0], gramR.at[0], ypeer)
    g_one.start()
    gram(rows_h, piece_a)

    def x_dev(j):
        return (dp, ((x + j) % 4) * 2 + yh)

    def a_one(j):
        return remote(GSA.at[(x + j) % 4], RA1.at[x], gramS.at[j], gramR.at[j], x_dev(j))

    def g_two(j):
        return remote(G2.at[(x + j) % 4], RG2.at[x], gramS.at[3 + j], gramR.at[3 + j], x_dev(j))

    for j in (2, 1, 3):
        a_one(j).start()
    h_sib = remote(H.at[c], H.at[c], hx.at[0], hx.at[1], sib)
    h_sib.start()

    for e in range(EX):
        tr = gin[e * SEQ : (e + 1) * SEQ, :].T
        gT[:, :, :, e * SEQ : (e + 1) * SEQ] = tr.reshape(2, PH, RW, SEQ)
    g_local = pltpu.make_async_copy(gT.at[c], Gb.at[:, t, c], gl)
    g_sib = remote(gT.at[oc], Gb.at[:, t, c], gx.at[0], gx.at[1], sib)
    g_local.start()
    g_sib.start()

    g_one.wait_recv()
    G2[...] = GSG[yh] + RG1[...]
    for j in (2, 1, 3):
        g_two(j).start()
    g_local.wait()
    g_sib.wait()
    for k in range(2):
        own_y(k).start()
    for j in range(1, 4):
        a_one(j).wait_recv()
    RA1[x] = GSA[x]
    A2[...] = (RA1[0] + RA1[1]) + (RA1[2] + RA1[3])
    a_two = remote(A2.at[1 - yh], RA2, gramS.at[7], gramR.at[7], ypeer)
    a_two.start()
    start_own_x(0)
    for j in range(1, 4):
        g_two(j).wait_recv()
    RG2[x] = G2[x]
    grad_gram = (RG2[0] + RG2[1]) + (RG2[2] + RG2[3])
    a_two.wait_recv()
    prod = (A2[yh] + RA2[...]) * grad_gram

    r32 = lax.broadcasted_iota(jnp.int32, (32, LANES), 0)
    l32 = lax.broadcasted_iota(jnp.int32, (32, LANES), 1)
    weight = jnp.where(l32 == r32 + t * 32, 1.0, 2.0)
    l8 = lax.broadcasted_iota(jnp.int32, (8, LANES), 1)
    mine = jnp.where(l8 // 16 == t, prod[EX * 32 :], 0.0)
    for e in range(EX):
        part = jnp.sum(prod[e * 32 : (e + 1) * 32] * weight, axis=0, keepdims=True)
        mine = mine + jnp.where(e8 == e, part, 0.0)
    SQm[...] = mine
    SQ[t] = mine

    def sq_copy(j):
        peer = (t + j) % 8
        return remote(SQm, SQ.at[t], sqS.at[j], sqR.at[j], (dp, peer))

    for j in range(1, 8):
        sq_copy(j).start()
    start_peer_x(0)
    own_y(2).start()
    start_own_x(1)
    for j in range(1, 8):
        sq_copy(j).wait_recv()
    sq = SQ[0]
    for s in range(1, 8):
        sq = sq + SQ[s]
    sq = jnp.sum(sq, axis=1, keepdims=True)
    bound = jnp.float32(0.15) * jnp.sqrt(jnp.float32(SEQ) * FF * D)
    factor = jnp.minimum(1.0, bound / jnp.sqrt(jnp.maximum(sq, 0.0) + 1e-06))
    FAC[c] = jnp.broadcast_to(factor, (8, 256))
    fac_sib = remote(FAC.at[c], FAC.at[c], facx.at[0], facx.at[1], sib)
    fac_sib.start()
    start_fwd_x(0)
    start_peer_x(1)
    h_sib.wait()
    fac_sib.wait()
    g_one.wait_send()
    a_two.wait_send()
    for j in range(1, 4):
        a_one(j).wait_send()
        g_two(j).wait_send()
    for j in range(1, 8):
        sq_copy(j).wait_send()

    def compute(k, s):
        def block(n):
            cols = pl.ds(pl.multiple_of(n * 256, 256), 256)
            acc = None
            for e in range(2 * EX):
                cs, j = divmod(e, EX)
                lhs = Gb[k, :, cs, :, j * SEQ : (j + 1) * SEQ].reshape(8 * RW, SEQ)
                rhs = H[cs, j * SEQ : (j + 1) * SEQ, cols]
                d = jnp.dot(lhs, rhs, preferred_element_type=F32) * FAC[cs, j : j + 1, :]
                acc = d if acc is None else acc + d
            return acc.reshape(4, 2, RW, 256)

        def to_z(n, carry):
            Pz[s, :, :, :, pl.ds(pl.multiple_of(n * 256, 256), 256)] = block(n)
            return carry

        def to_y(n, carry):
            r = block(n + ZB)
            for b in range(2):
                Py[s, b, :, n] = r[:, b]
            return carry

        lax.fori_loop(0, 2, to_y, 0)
        y1_copy(k).start()
        lax.fori_loop(0, ZB, to_z, 0)

    def pick(d, kind):
        if kind == 0:
            return zo, d
        if kind == 1:
            return (zp, 1) if d == 0 else (zm, 0)
        return (zp, 0) if d == 0 else (zm, 1)

    def z_copy(k, d, kind):
        s = k % SLOTS
        a, b = pick(d, kind)
        return remote(
            Pz.at[s, a, b], ZR.at[k, d, kind], zsnd.at[s, 2 * kind + d], zrcv.at[k, d, kind], up if d == 0 else down
        )

    def y_copy(k):
        s = k % SLOTS
        return remote(Pz.at[s, z, 1 - yl], YR.at[k], zsnd.at[s, 6], yrcv.at[k], ylo)

    def y1_copy(k):
        s = k % SLOTS
        return remote(Py.at[s, 1 - yl], YZ.at[k], wsnd.at[s, 6], y1rcv.at[k], ylo)

    def w_copy(k, d, kind):
        s = k % SLOTS
        a, b = pick(d, kind)
        return remote(
            Py.at[s, yl, a, b], WR.at[k, d, kind], wsnd.at[s, 2 * kind + d], wrcv.at[k, d, kind], up if d == 0 else down
        )

    def out_copy(k):
        return pltpu.make_async_copy(OS.at[k], out.at[pl.ds(pl.multiple_of(k * RW, RW), RW)], osem.at[k])

    def send_first(copy, k):
        for kind in range(2):
            for d in range(2):
                copy(k, d, kind).start()

    def z_relay(k):
        s = k % SLOTS
        for d in range(2):
            z_copy(k, d, 0).wait_recv()
            a, b = pick(d, 2)
            Pz[s, a, b] = Pz[s, a, b] + ZR[k, d, 0]
            z_copy(k, d, 2).start()

    def w_first(k):
        s = k % SLOTS
        y1_copy(k).wait_recv()
        Py[s, yl] = Py[s, yl] + YZ[k]
        send_first(w_copy, k)

    def w_relay(k):
        s = k % SLOTS
        for d in range(2):
            w_copy(k, d, 0).wait_recv()
            a, b = pick(d, 2)
            Py[s, yl, a, b] = Py[s, yl, a, b] + WR[k, d, 0]
            w_copy(k, d, 2).start()

    def z_last(k):
        s = k % SLOTS
        for kind in (1, 2):
            for d in range(2):
                z_copy(k, d, kind).wait_recv()
        Pz[s, z, 0] = Pz[s, z, 0] + ZR[k, 0, 2] + ZR[k, 1, 1]
        Pz[s, z, 1] = Pz[s, z, 1] + ZR[k, 0, 1] + ZR[k, 1, 2]
        y_copy(k).start()

    def finish(k):
        s = k % SLOTS
        for kind in (1, 2):
            for d in range(2):
                w_copy(k, d, kind).wait_recv()
        OS[k, :, ZC : ZC + 256] = Py[s, yl, z, 0] + WR[k, 0, 2] + WR[k, 1, 1]
        OS[k, :, ZC + 256 :] = Py[s, yl, z, 1] + WR[k, 0, 1] + WR[k, 1, 2]
        y_copy(k).wait_recv()
        OS[k, :, :ZC] = Pz[s, z, yl] + YR[k]
        out_copy(k).start()

    def free(k):
        for kind in range(3):
            for d in range(2):
                z_copy(k, d, kind).wait_send()
                w_copy(k, d, kind).wait_send()
        y_copy(k).wait_send()
        y1_copy(k).wait_send()

    def step(k, carry):
        @pl.when(k < PH)
        def _():
            wait_rest(k)

            @pl.when(k >= SLOTS)
            def _():
                free(k - SLOTS)

            compute(k, k % SLOTS)
            send_first(z_copy, k)

        @pl.when((k >= 1) & (k < PH + 1))
        def _():
            z_relay(k - 1)

        @pl.when(k + 3 < PH)
        def _():
            own_y(k + 3).start()

        @pl.when(k + 2 < PH)
        def _():
            start_own_x(k + 2)

        @pl.when(k + 1 < PH)
        def _():
            start_fwd_x(k + 1)

        @pl.when(k + 2 < PH)
        def _():
            start_peer_x(k + 2)

        @pl.when((k >= 1) & (k < PH + 1))
        def _():
            w_first(k - 1)

        @pl.when((k >= 2) & (k < PH + 2))
        def _():
            z_last(k - 2)
            w_relay(k - 2)

        @pl.when(k >= 3)
        def _():
            finish(k - 3)

        return carry

    lax.fori_loop(0, PH + 3, step, 0)

    def drain(k, carry):
        own_y(k).wait_send()
        for d in range(2):
            own_x(k, d).wait_send()
            peer_x(k, d).wait_send()
            fwd_x(k, d).wait_send()
        out_copy(k).wait()
        return carry

    lax.fori_loop(0, PH, drain, 0)
    lax.fori_loop(PH - SLOTS, PH, lambda k, carry: (free(k), carry)[1], 0)


def per_device(activations, out_grads, noise):
    dma = pltpu.SemaphoreType.DMA
    summed = pl.pallas_call(
        kernel,
        out_shape=jax.ShapeDtypeStruct((256, FL), F32),
        in_specs=[pl.BlockSpec(memory_space=pl.ANY)] * 2,
        out_specs=pl.BlockSpec(memory_space=pl.ANY),
        scratch_shapes=[
            pltpu.VMEM((2, TOK, FL), BF16),
            pltpu.VMEM((TOK, DL), BF16),
            pltpu.VMEM((2, PH, RW, TOK), BF16),
            pltpu.VMEM((PH, 8, 2, RW, TOK), BF16),
            pltpu.VMEM((4, 2, GROWS, LANES), F32),
            pltpu.VMEM((2, 4, GROWS, LANES), F32),
            pltpu.VMEM((4, 2, GROWS, LANES), F32),
            pltpu.VMEM((2, GROWS, LANES), F32),
            pltpu.VMEM((GROWS, LANES), F32),
            pltpu.VMEM((4, GROWS, LANES), F32),
            pltpu.VMEM((4, GROWS, LANES), F32),
            pltpu.VMEM((4, GROWS, LANES), F32),
            pltpu.VMEM((8, LANES), F32),
            pltpu.VMEM((8, 8, LANES), F32),
            pltpu.VMEM((2, 8, 256), F32),
            pltpu.VMEM((SLOTS, 4, 2, RW, ZC), F32),
            pltpu.VMEM((SLOTS, 2, 4, 2, RW, 256), F32),
            pltpu.VMEM((PH, 2, 3, RW, ZC), F32),
            pltpu.VMEM((PH, RW, ZC), F32),
            pltpu.VMEM((PH, 4, 2, RW, 256), F32),
            pltpu.VMEM((PH, 2, 3, RW, 256), F32),
            pltpu.VMEM((PH, RW, FL), F32),
            dma((EX,)),
            dma,
            dma((2,)),
            dma((2,)),
            dma,
            dma((8,)),
            dma((8,)),
            dma((8,)),
            dma((8,)),
            dma((2,)),
            dma((PH, 7)),
            dma((PH, 2, 3)),
            dma((PH,)),
            dma((SLOTS, 7)),
            dma((PH, 2, 3)),
            dma((PH,)),
            dma((SLOTS, 7)),
            dma((PH, 2, 3)),
            dma((PH,)),
            dma((PH,)),
        ],
        compiler_params=pltpu.CompilerParams(
            collective_id=0, has_side_effects=True, vmem_limit_bytes=62 << 20
        ),
        cost_estimate=pl.CostEstimate(flops=24 * 10**9, bytes_accessed=9 * 10**6, transcendentals=0),
    )(activations, out_grads)
    return (summed + noise) / COUNT


def solution(mesh):
    return jax.shard_map(
        per_device,
        mesh=mesh,
        in_specs=(P("dp", "tensor"), P("dp", "tensor"), P("dp", "tensor")),
        out_specs=P("dp", "tensor"),
        check_vma=False,
    )
```

```python
import functools

import jax
import jax.numpy as jnp
from jax import lax
from jax.experimental import pallas as pl
from jax.experimental.pallas import tpu as pltpu
from jax.sharding import PartitionSpec as P

MESH = pl.DeviceIdType.MESH
F32 = jnp.float32
BF16 = jnp.bfloat16
D = 4096
FF = 14336
SEQ = 256
EX = 6
TOK = EX * SEQ
FL = 1792
DL = 512
PH = 16
RW = 16
GP = 9
SLOTS = 4
ZB = 5
ZC = ZB * 256
MC = ZC + 256
GROWS = EX * 32 + 8
COUNT = 96
LANES = 128


class Single(int):
    pass


def kernel(
    act, g, out,
    H, gin, gT, Gb, GSA, GSG, RA1, A2, RA2, RG1, G2, RG2, SQm, SQ, FAC, Pz, Py, ZR, YR, YZ, OS,
    hsem, gsem, hx, gx, gl, gramS, gramR, sqS, sqR, facx, gsnd, grcv, gy, zsnd, zrcv, yrcv, y1rcv, osem,
):
    dp = lax.axis_index("dp")
    t = lax.axis_index("tensor")
    z, yl, c = dp // 4, (dp // 2) % 2, dp % 2
    x, yh = t // 2, t % 2
    oc = 1 - c
    sib = (z * 4 + yl * 2 + oc, t)
    xp, xm = (x + 1) % 4, (x + 3) % 4
    right = (dp, xp * 2 + yh)
    left = (dp, xm * 2 + yh)
    ypeer = (dp, x * 2 + 1 - yh)
    zp, zm, zo = (z + 1) % 4, (z + 3) % 4, (z + 2) % 4
    up = (zp * 4 + yl * 2 + c, t)
    down = (zm * 4 + yl * 2 + c, t)
    ylo = (z * 4 + (1 - yl) * 2 + c, t)

    def remote(src, dst, ssem, rsem, dev):
        return pltpu.make_async_remote_copy(
            src_ref=src, dst_ref=dst, send_sem=ssem, recv_sem=rsem, device_id=dev, device_id_type=MESH
        )

    g_in = pltpu.make_async_copy(g, gin, gsem)
    g_in.start()

    def h_in(e):
        rows = pl.ds(e * SEQ, SEQ)
        return pltpu.make_async_copy(act.at[rows], H.at[c, rows], hsem.at[e])

    for e in range(EX):
        h_in(e).start()

    barrier = pltpu.get_barrier_semaphore()
    partners = [(dp, (t + j) % 8) for j in range(1, 8)] + [sib, up, down, ylo]
    for dev in partners:
        pl.semaphore_signal(barrier, inc=1, device_id=dev, device_id_type=MESH)

    def shard_copy(k, owner, ssem, rsem, dev):
        if isinstance(k, Single):
            part = Gb.at[pl.ds(2 * k - k // 8, 1), owner]
        else:
            part = Gb.at[pl.ds(2 * k - 1, 2), owner]
        return remote(part, part, ssem, rsem, dev)

    def own_y(k):
        return shard_copy(k, t, gsnd.at[k, 0], gy.at[k], ypeer)

    def own_x(k, d):
        return shard_copy(k, t, gsnd.at[k, 1 + d], grcv.at[k, d, 0], right if d == 0 else left)

    def peer_x(k, d):
        return shard_copy(k, x * 2 + 1 - yh, gsnd.at[k, 3 + d], grcv.at[k, d, 1], right if d == 0 else left)

    def fwd_x(k, d):
        owner = xm * 2 if d == 0 else xp * 2 + 1
        return shard_copy(k, owner, gsnd.at[k, 5 + d], grcv.at[k, d, 2], right if d == 0 else left)

    def wait_shard(k, d, kind):
        shard_copy(k, t, gsnd.at[k, 0], grcv.at[k, d, kind], ypeer).wait_recv()

    def start_own_x(k):
        own_x(k, 0).start()
        own_x(k, 1).start()

    def start_peer_x(k):
        own_y(k).wait_recv()
        peer_x(k, 0).start()
        peer_x(k, 1).start()

    def start_fwd_x(k):
        wait_shard(k, 0, yh)
        fwd_x(k, 0).start()
        wait_shard(k, 1, 1 - yh)
        fwd_x(k, 1).start()

    def wait_rest(k):
        wait_shard(k, 0, 1 - yh)
        wait_shard(k, 1, yh)
        wait_shard(k, 0, 2)
        wait_shard(k, 1, 2)

    i0 = lax.broadcasted_iota(jnp.int32, (LANES, LANES), 0)
    i1 = lax.broadcasted_iota(jnp.int32, (LANES, LANES), 1)
    e8 = lax.broadcasted_iota(jnp.int32, (8, LANES), 0)
    nt = (((1,), (1,)), ((), ()))
    zero8 = jnp.zeros((8, LANES), F32)

    def gram(rows_of, piece):
        def one(e, diags):
            r = rows_of(e, pl.ds(pl.multiple_of(e * SEQ, SEQ), SEQ))
            a = lax.dot_general(r, r, nt, preferred_element_type=F32)
            packed = jnp.where(i0 >= i1, a[:LANES, :LANES], a[LANES:, LANES:])
            below = a[LANES:, :LANES]
            for owner in range(8):
                part = packed if owner < 4 else below
                lo = (owner % 4) * 32
                piece(owner, pl.ds(pl.multiple_of(e * 32, 32), 32), part[lo : lo + 32])
            diag = jnp.sum(jnp.where(i0 == i1, a[LANES:, LANES:], 0.0), axis=0, keepdims=True)
            return jnp.where(e8 == e, diag, diags)

        diags = lax.fori_loop(0, EX, one, zero8)
        for owner in range(8):
            piece(owner, slice(EX * 32, GROWS), diags)

    def piece_a(owner, rows, value):
        GSA[owner // 2, owner % 2, rows, :] = value

    def piece_g(owner, rows, value):
        GSG[owner % 2, owner // 2, rows, :] = value

    def rows_h(e, rows):
        h_in(e).wait()
        return H[c, rows, :]

    g_in.wait()
    for e in range(EX):
        tr = gin[e * SEQ : (e + 1) * SEQ, :].T
        gT[:, :, :, e * SEQ : (e + 1) * SEQ] = tr.reshape(2, PH, RW, SEQ)
    g_local = pltpu.make_async_copy(gT.at[c], Gb.at[:, t, c], gl)
    g_local.start()
    pl.semaphore_wait(barrier, len(partners))
    g_sib = remote(gT.at[oc], Gb.at[:, t, c], gx.at[0], gx.at[1], sib)
    g_sib.start()
    gram(lambda e, rows: gin[rows, :], piece_g)
    g_one = remote(GSG.at[1 - yh], RG1, gramS.at[0], gramR.at[0], ypeer)
    g_one.start()
    g_local.wait()
    g_sib.wait()
    own_y(Single(0)).start()
    start_own_x(Single(0))
    gram(rows_h, piece_a)

    def x_dev(j):
        return (dp, ((x + j) % 4) * 2 + yh)

    def a_one(j):
        return remote(GSA.at[(x + j) % 4], RA1.at[x], gramS.at[j], gramR.at[j], x_dev(j))

    def g_two(j):
        return remote(G2.at[(x + j) % 4], RG2.at[x], gramS.at[3 + j], gramR.at[3 + j], x_dev(j))

    for j in (2, 1, 3):
        a_one(j).start()
    h_sib = remote(H.at[c], H.at[c], hx.at[0], hx.at[1], sib)
    h_sib.start()

    g_one.wait_recv()
    G2[...] = GSG[yh] + RG1[...]
    for j in (2, 1, 3):
        g_two(j).start()
    start_peer_x(Single(0))
    for j in range(1, 4):
        a_one(j).wait_recv()
    RA1[x] = GSA[x]
    A2[...] = (RA1[0] + RA1[1]) + (RA1[2] + RA1[3])
    a_two = remote(A2.at[1 - yh], RA2, gramS.at[7], gramR.at[7], ypeer)
    a_two.start()
    start_own_x(1)
    for j in range(1, 4):
        g_two(j).wait_recv()
    RG2[x] = G2[x]
    grad_gram = (RG2[0] + RG2[1]) + (RG2[2] + RG2[3])
    a_two.wait_recv()
    prod = (A2[yh] + RA2[...]) * grad_gram

    r32 = lax.broadcasted_iota(jnp.int32, (32, LANES), 0)
    l32 = lax.broadcasted_iota(jnp.int32, (32, LANES), 1)
    weight = jnp.where(l32 == r32 + t * 32, 1.0, 2.0)
    l8 = lax.broadcasted_iota(jnp.int32, (8, LANES), 1)
    mine = jnp.where(l8 // 16 == t, prod[EX * 32 :], 0.0)
    for e in range(EX):
        part = jnp.sum(prod[e * 32 : (e + 1) * 32] * weight, axis=0, keepdims=True)
        mine = mine + jnp.where(e8 == e, part, 0.0)
    SQm[...] = mine
    SQ[t] = mine

    def sq_copy(j):
        peer = (t + j) % 8
        return remote(SQm, SQ.at[t], sqS.at[j], sqR.at[j], (dp, peer))

    for j in range(1, 8):
        sq_copy(j).start()
    start_fwd_x(Single(0))
    for k in range(1, 4):
        own_y(k).start()
    for j in range(1, 8):
        sq_copy(j).wait_recv()
    sq = SQ[0]
    for s in range(1, 8):
        sq = sq + SQ[s]
    sq = jnp.sum(sq, axis=1, keepdims=True)
    bound = jnp.float32(0.15) * jnp.sqrt(jnp.float32(SEQ) * FF * D)
    factor = jnp.minimum(1.0, bound / jnp.sqrt(jnp.maximum(sq, 0.0) + 1e-06))
    FAC[c] = jnp.broadcast_to(factor, (8, 256))
    fac_sib = remote(FAC.at[c], FAC.at[c], facx.at[0], facx.at[1], sib)
    fac_sib.start()
    start_peer_x(1)
    start_own_x(2)
    h_sib.wait()
    fac_sib.wait()
    g_one.wait_send()
    a_two.wait_send()
    for j in range(1, 4):
        a_one(j).wait_send()
        g_two(j).wait_send()
    for j in range(1, 8):
        sq_copy(j).wait_send()

    def block(k, n):
        cols = pl.ds(pl.multiple_of(n * 256, 256), 256)
        acc = None
        for e in range(2 * EX):
            cs, j = divmod(e, EX)
            lhs = Gb[k, :, cs, :, j * SEQ : (j + 1) * SEQ].reshape(8 * RW, SEQ)
            rhs = H[cs, j * SEQ : (j + 1) * SEQ, cols]
            d = jnp.dot(lhs, rhs, preferred_element_type=F32) * FAC[cs, j : j + 1, :]
            acc = d if acc is None else acc + d
        return acc.reshape(4, 2, RW, 256)

    def compute_y(k):
        def one(n, carry):
            r = block(k, n + ZB)
            for b in range(2):
                Py[k % SLOTS, b, :, n] = r[:, b]
            return carry

        lax.fori_loop(0, 2, one, 0)

    def compute_z(k):
        def one(n, carry):
            Pz[k % SLOTS, :, :, :, pl.ds(pl.multiple_of(n * 256, 256), 256)] = block(k, n)
            return carry

        lax.fori_loop(0, ZB, one, 0)

    def pick(d, kind):
        if kind == 0:
            return zo, d
        if kind == 1:
            return (zp, 1) if d == 0 else (zm, 0)
        return (zp, 0) if d == 0 else (zm, 1)

    def z_copy(k, d, kind, cols=slice(0, MC)):
        s = k % SLOTS
        a, b = pick(d, kind)
        return remote(
            Pz.at[s, a, b, :, cols],
            ZR.at[k, d, kind, :, cols],
            zsnd.at[s, 2 * kind + d],
            zrcv.at[k, d, kind],
            up if d == 0 else down,
        )

    late = slice(ZC, MC)

    def y_copy(k):
        s = k % SLOTS
        return remote(Pz.at[s, z, 1 - yl, :, 0:ZC], YR.at[k], zsnd.at[s, 6], yrcv.at[k], ylo)

    def y1_copy(k):
        s = k % SLOTS
        return remote(Py.at[s, 1 - yl], YZ.at[k], zsnd.at[s, 7], y1rcv.at[k], ylo)

    def out_copy(k):
        return pltpu.make_async_copy(OS.at[k], out.at[pl.ds(pl.multiple_of(k * RW, RW), RW)], osem.at[k])

    def add_y1(k):
        y1_copy(k).wait_recv()
        Pz[(k + 1) % SLOTS, :, :, :, late] = Py[k % SLOTS, yl] + YZ[k]

    def z_first(k, cols):
        for kind in range(2):
            for d in range(2):
                z_copy(k, d, kind, cols).start()

    def z_relay(k, cols):
        s = k % SLOTS
        for d in range(2):
            z_copy(k, d, 0, cols).wait_recv()
            a, b = pick(d, 2)
            Pz[s, a, b, :, cols] = Pz[s, a, b, :, cols] + ZR[k, d, 0, :, cols]
            z_copy(k, d, 2, cols).start()

    def z_wait(k, cols):
        for kind in (1, 2):
            for d in range(2):
                z_copy(k, d, kind, cols).wait_recv()

    def z_sum(k, b, cols):
        one, two = (2, 1) if b == 0 else (1, 2)
        return Pz[k % SLOTS, z, b, :, cols] + ZR[k, 0, one, :, cols] + ZR[k, 1, two, :, cols]

    def store_late(k):
        for b in range(2):
            OS[k - 1, :, ZC + 256 * b : ZC + 256 * (b + 1)] = z_sum(k, b, late)

    def z_last(k):
        z_wait(k, slice(0, MC))
        for b in range(2):
            Pz[k % SLOTS, z, b, :, 0:ZC] = z_sum(k, b, slice(0, ZC))
        y_copy(k).start()

        @pl.when(k >= 1)
        def _():
            store_late(k)

    def finish(k):
        s = k % SLOTS
        y_copy(k).wait_recv()
        OS[k, :, 0:ZC] = Pz[s, z, yl, :, 0:ZC] + YR[k]
        out_copy(k).start()

    def free(k):
        for kind in range(3):
            for d in range(2):
                z_copy(k, d, kind).wait_send()
        y_copy(k).wait_send()
        y1_copy(k).wait_send()

    Pz[0, :, :, :, late] = jnp.zeros((4, 2, RW, MC - ZC), F32)

    def step(k, carry):
        j = k // 2
        even = k % 2 == 0

        @pl.when((~even) & (k < PH - 1))
        def _():
            wait_rest(j + 1)

        for p, now in ((0, 0), (8, PH - 1)):

            @pl.when(k == now)
            def _():
                wait_rest(Single(p))

        @pl.when((k >= SLOTS) & (k <= PH))
        def _():
            free(k - SLOTS)

        @pl.when(k < PH)
        def _():
            compute_y(k)
            y1_copy(k).start()
            compute_z(k)

        @pl.when((k >= 1) & (k <= PH))
        def _():
            add_y1(k - 1)

        @pl.when(k < PH)
        def _():
            z_first(k, slice(0, MC))

        @pl.when(k == PH)
        def _():
            z_first(k, late)

        @pl.when((k >= 1) & (k <= PH))
        def _():
            z_relay(k - 1, slice(0, MC))

        @pl.when(k == PH + 1)
        def _():
            z_relay(PH, late)

        @pl.when(k == 0)
        def _():
            start_fwd_x(1)
            start_peer_x(2)

        def at(when, op, ahead, last):
            @pl.when(when & (j + ahead < GP - 1))
            def _():
                op(j + ahead)

            @pl.when(k == last)
            def _():
                op(Single(GP - 1))

        at(~even, start_fwd_x, 2, 13)
        at(~even, start_peer_x, 3, 11)
        at(even, start_own_x, 3, 10)
        at(even, lambda p: own_y(p).start(), 4, 8)

        @pl.when((k >= 2) & (k <= PH + 1))
        def _():
            z_last(k - 2)

        @pl.when(k == PH + 2)
        def _():
            z_wait(PH, late)
            store_late(PH)

        @pl.when(k >= 3)
        def _():
            finish(k - 3)

        return carry

    lax.fori_loop(0, PH + 3, step, 0)

    def drain(k, carry):
        own_y(k).wait_send()
        for d in range(2):
            own_x(k, d).wait_send()
            peer_x(k, d).wait_send()
            fwd_x(k, d).wait_send()
        return carry

    lax.fori_loop(1, GP - 1, drain, 0)
    drain(Single(0), 0)
    drain(Single(GP - 1), 0)
    lax.fori_loop(PH - SLOTS + 1, PH, lambda k, carry: (free(k), carry)[1], 0)
    for kind in range(3):
        for d in range(2):
            z_copy(PH, d, kind, late).wait_send()
    lax.fori_loop(0, PH, lambda k, carry: (out_copy(k).wait(), carry)[1], 0)


def per_device(activations, out_grads, noise):
    dma = pltpu.SemaphoreType.DMA
    summed = pl.pallas_call(
        kernel,
        out_shape=jax.ShapeDtypeStruct((256, FL), F32),
        in_specs=[pl.BlockSpec(memory_space=pl.ANY)] * 2,
        out_specs=pl.BlockSpec(memory_space=pl.ANY),
        scratch_shapes=[
            pltpu.VMEM((2, TOK, FL), BF16),
            pltpu.VMEM((TOK, DL), BF16),
            pltpu.VMEM((2, PH, RW, TOK), BF16),
            pltpu.VMEM((PH, 8, 2, RW, TOK), BF16),
            pltpu.VMEM((4, 2, GROWS, LANES), F32),
            pltpu.VMEM((2, 4, GROWS, LANES), F32),
            pltpu.VMEM((4, 2, GROWS, LANES), F32),
            pltpu.VMEM((2, GROWS, LANES), F32),
            pltpu.VMEM((GROWS, LANES), F32),
            pltpu.VMEM((4, GROWS, LANES), F32),
            pltpu.VMEM((4, GROWS, LANES), F32),
            pltpu.VMEM((4, GROWS, LANES), F32),
            pltpu.VMEM((8, LANES), F32),
            pltpu.VMEM((8, 8, LANES), F32),
            pltpu.VMEM((2, 8, 256), F32),
            pltpu.VMEM((SLOTS, 4, 2, RW, MC), F32),
            pltpu.VMEM((SLOTS, 2, 4, 2, RW, 256), F32),
            pltpu.VMEM((PH + 1, 2, 3, RW, MC), F32),
            pltpu.VMEM((PH, RW, ZC), F32),
            pltpu.VMEM((PH, 4, 2, RW, 256), F32),
            pltpu.VMEM((PH, RW, FL), F32),
            dma((EX,)),
            dma,
            dma((2,)),
            dma((2,)),
            dma,
            dma((8,)),
            dma((8,)),
            dma((8,)),
            dma((8,)),
            dma((2,)),
            dma((GP, 7)),
            dma((GP, 2, 3)),
            dma((GP,)),
            dma((SLOTS, 8)),
            dma((PH + 1, 2, 3)),
            dma((PH,)),
            dma((PH,)),
            dma((PH,)),
        ],
        compiler_params=pltpu.CompilerParams(
            collective_id=0, has_side_effects=True, vmem_limit_bytes=62 << 20
        ),
        cost_estimate=pl.CostEstimate(flops=24 * 10**9, bytes_accessed=9 * 10**6, transcendentals=0),
    )(activations, out_grads)
    return (summed + noise) / COUNT


def solution(mesh):
    return jax.shard_map(
        per_device,
        mesh=mesh,
        in_specs=(P("dp", "tensor"), P("dp", "tensor"), P("dp", "tensor")),
        out_specs=P("dp", "tensor"),
        check_vma=False,
    )
```

```python
import functools

import jax
import jax.numpy as jnp
from jax import lax
from jax.experimental import pallas as pl
from jax.experimental.pallas import tpu as pltpu
from jax.sharding import PartitionSpec as P

MESH = pl.DeviceIdType.MESH
F32 = jnp.float32
BF16 = jnp.bfloat16
D = 4096
FF = 14336
SEQ = 256
EX = 6
TOK = EX * SEQ
FL = 1792
DL = 512
PH = 16
RW = 16
SLOTS = 4
ZB = 5
ZC = ZB * 256
MC = ZC + 256
GROWS = EX * 32 + 8
COUNT = 96
LANES = 128


def kernel(
    act, g, out,
    H, gin, gT, Gb, GSA, GSG, RA1, A2, RA2, RG1, G2, RG2, SQm, SQ, FAC, Pz, Py, ZR, YR, YZ, OS,
    hsem, gsem, hx, gx, gl, gramS, gramR, sqS, sqR, facx, gsnd, grcv, gy, zsnd, zrcv, yrcv, y1rcv, osem,
):
    dp = lax.axis_index("dp")
    t = lax.axis_index("tensor")
    z, yl, c = dp // 4, (dp // 2) % 2, dp % 2
    x, yh = t // 2, t % 2
    oc = 1 - c
    sib = (z * 4 + yl * 2 + oc, t)
    xp, xm = (x + 1) % 4, (x + 3) % 4
    right = (dp, xp * 2 + yh)
    left = (dp, xm * 2 + yh)
    ypeer = (dp, x * 2 + 1 - yh)
    zp, zm, zo = (z + 1) % 4, (z + 3) % 4, (z + 2) % 4
    up = (zp * 4 + yl * 2 + c, t)
    down = (zm * 4 + yl * 2 + c, t)
    ylo = (z * 4 + (1 - yl) * 2 + c, t)

    def remote(src, dst, ssem, rsem, dev):
        return pltpu.make_async_remote_copy(
            src_ref=src, dst_ref=dst, send_sem=ssem, recv_sem=rsem, device_id=dev, device_id_type=MESH
        )

    g_in = pltpu.make_async_copy(g, gin, gsem)
    g_in.start()

    def h_in(e):
        rows = pl.ds(e * SEQ, SEQ)
        return pltpu.make_async_copy(act.at[rows], H.at[c, rows], hsem.at[e])

    for e in range(EX):
        h_in(e).start()

    barrier = pltpu.get_barrier_semaphore()
    partners = [(dp, (t + j) % 8) for j in range(1, 8)] + [sib, up, down, ylo]
    for dev in partners:
        pl.semaphore_signal(barrier, inc=1, device_id=dev, device_id_type=MESH)

    def shard_copy(k, owner, ssem, rsem, dev):
        part = Gb.at[k, owner]
        return remote(part, part, ssem, rsem, dev)

    def own_y(k):
        return shard_copy(k, t, gsnd.at[k, 0], gy.at[k], ypeer)

    def own_x(k, d):
        return shard_copy(k, t, gsnd.at[k, 1 + d], grcv.at[k, d, 0], right if d == 0 else left)

    def peer_x(k, d):
        return shard_copy(k, x * 2 + 1 - yh, gsnd.at[k, 3 + d], grcv.at[k, d, 1], right if d == 0 else left)

    def fwd_x(k, d):
        owner = xm * 2 if d == 0 else xp * 2 + 1
        return shard_copy(k, owner, gsnd.at[k, 5 + d], grcv.at[k, d, 2], right if d == 0 else left)

    def wait_shard(k, d, kind):
        shard_copy(k, t, gsnd.at[k, 0], grcv.at[k, d, kind], ypeer).wait_recv()

    def start_own_x(k):
        own_x(k, 0).start()
        own_x(k, 1).start()

    def start_peer_x(k):
        own_y(k).wait_recv()
        peer_x(k, 0).start()
        peer_x(k, 1).start()

    def start_fwd_x(k):
        wait_shard(k, 0, yh)
        fwd_x(k, 0).start()
        wait_shard(k, 1, 1 - yh)
        fwd_x(k, 1).start()

    def wait_rest(k):
        wait_shard(k, 0, 1 - yh)
        wait_shard(k, 1, yh)
        wait_shard(k, 0, 2)
        wait_shard(k, 1, 2)

    i0 = lax.broadcasted_iota(jnp.int32, (LANES, LANES), 0)
    i1 = lax.broadcasted_iota(jnp.int32, (LANES, LANES), 1)
    e8 = lax.broadcasted_iota(jnp.int32, (8, LANES), 0)
    nt = (((1,), (1,)), ((), ()))
    zero8 = jnp.zeros((8, LANES), F32)

    def gram(rows_of, piece):
        def one(e, diags):
            r = rows_of(e, pl.ds(pl.multiple_of(e * SEQ, SEQ), SEQ))
            a = lax.dot_general(r, r, nt, preferred_element_type=F32)
            packed = jnp.where(i0 >= i1, a[:LANES, :LANES], a[LANES:, LANES:])
            below = a[LANES:, :LANES]
            for owner in range(8):
                part = packed if owner < 4 else below
                lo = (owner % 4) * 32
                piece(owner, pl.ds(pl.multiple_of(e * 32, 32), 32), part[lo : lo + 32])
            diag = jnp.sum(jnp.where(i0 == i1, a[LANES:, LANES:], 0.0), axis=0, keepdims=True)
            return jnp.where(e8 == e, diag, diags)

        diags = lax.fori_loop(0, EX, one, zero8)
        for owner in range(8):
            piece(owner, slice(EX * 32, GROWS), diags)

    def piece_a(owner, rows, value):
        GSA[owner // 2, owner % 2, rows, :] = value

    def piece_g(owner, rows, value):
        GSG[owner % 2, owner // 2, rows, :] = value

    def rows_h(e, rows):
        h_in(e).wait()
        return H[c, rows, :]

    g_in.wait()
    for e in range(EX):
        tr = gin[e * SEQ : (e + 1) * SEQ, :].T
        gT[:, :, :, e * SEQ : (e + 1) * SEQ] = tr.reshape(2, PH, RW, SEQ)
    g_local = pltpu.make_async_copy(gT.at[c], Gb.at[:, t, c], gl)
    g_local.start()
    pl.semaphore_wait(barrier, len(partners))
    g_sib = remote(gT.at[oc], Gb.at[:, t, c], gx.at[0], gx.at[1], sib)
    g_sib.start()
    gram(lambda e, rows: gin[rows, :], piece_g)
    g_one = remote(GSG.at[1 - yh], RG1, gramS.at[0], gramR.at[0], ypeer)
    g_one.start()
    g_local.wait()
    g_sib.wait()
    own_y(0).start()
    start_own_x(0)
    gram(rows_h, piece_a)

    def x_dev(j):
        return (dp, ((x + j) % 4) * 2 + yh)

    def a_one(j):
        return remote(GSA.at[(x + j) % 4], RA1.at[x], gramS.at[j], gramR.at[j], x_dev(j))

    def g_two(j):
        return remote(G2.at[(x + j) % 4], RG2.at[x], gramS.at[3 + j], gramR.at[3 + j], x_dev(j))

    for j in (2, 1, 3):
        a_one(j).start()
    h_sib = remote(H.at[c], H.at[c], hx.at[0], hx.at[1], sib)
    h_sib.start()

    g_one.wait_recv()
    G2[...] = GSG[yh] + RG1[...]
    for j in (2, 1, 3):
        g_two(j).start()
    start_peer_x(0)
    for j in range(1, 4):
        a_one(j).wait_recv()
    RA1[x] = GSA[x]
    A2[...] = (RA1[0] + RA1[1]) + (RA1[2] + RA1[3])
    a_two = remote(A2.at[1 - yh], RA2, gramS.at[7], gramR.at[7], ypeer)
    a_two.start()
    start_own_x(1)
    for j in range(1, 4):
        g_two(j).wait_recv()
    RG2[x] = G2[x]
    grad_gram = (RG2[0] + RG2[1]) + (RG2[2] + RG2[3])
    a_two.wait_recv()
    prod = (A2[yh] + RA2[...]) * grad_gram

    r32 = lax.broadcasted_iota(jnp.int32, (32, LANES), 0)
    l32 = lax.broadcasted_iota(jnp.int32, (32, LANES), 1)
    weight = jnp.where(l32 == r32 + t * 32, 1.0, 2.0)
    l8 = lax.broadcasted_iota(jnp.int32, (8, LANES), 1)
    mine = jnp.where(l8 // 16 == t, prod[EX * 32 :], 0.0)
    for e in range(EX):
        part = jnp.sum(prod[e * 32 : (e + 1) * 32] * weight, axis=0, keepdims=True)
        mine = mine + jnp.where(e8 == e, part, 0.0)
    SQm[...] = mine
    SQ[t] = mine

    def sq_copy(j):
        peer = (t + j) % 8
        return remote(SQm, SQ.at[t], sqS.at[j], sqR.at[j], (dp, peer))

    for j in range(1, 8):
        sq_copy(j).start()
    start_fwd_x(0)
    for k in range(1, 4):
        own_y(k).start()
    for j in range(1, 8):
        sq_copy(j).wait_recv()
    sq = SQ[0]
    for s in range(1, 8):
        sq = sq + SQ[s]
    sq = jnp.sum(sq, axis=1, keepdims=True)
    bound = jnp.float32(0.15) * jnp.sqrt(jnp.float32(SEQ) * FF * D)
    factor = jnp.minimum(1.0, bound / jnp.sqrt(jnp.maximum(sq, 0.0) + 1e-06))
    FAC[c] = jnp.broadcast_to(factor, (8, 256))
    fac_sib = remote(FAC.at[c], FAC.at[c], facx.at[0], facx.at[1], sib)
    fac_sib.start()
    start_peer_x(1)
    start_own_x(2)
    h_sib.wait()
    fac_sib.wait()
    g_one.wait_send()
    a_two.wait_send()
    for j in range(1, 4):
        a_one(j).wait_send()
        g_two(j).wait_send()
    for j in range(1, 8):
        sq_copy(j).wait_send()

    def block(k, n):
        cols = pl.ds(pl.multiple_of(n * 256, 256), 256)
        acc = None
        for e in range(2 * EX):
            cs, j = divmod(e, EX)
            lhs = Gb[k, :, cs, :, j * SEQ : (j + 1) * SEQ].reshape(8 * RW, SEQ)
            rhs = H[cs, j * SEQ : (j + 1) * SEQ, cols]
            d = jnp.dot(lhs, rhs, preferred_element_type=F32) * FAC[cs, j : j + 1, :]
            acc = d if acc is None else acc + d
        return acc.reshape(4, 2, RW, 256)

    def compute_y(k):
        def one(n, carry):
            r = block(k, n + ZB)
            for b in range(2):
                Py[k % SLOTS, b, :, n] = r[:, b]
            return carry

        lax.fori_loop(0, 2, one, 0)

    def compute_z(k):
        def one(n, carry):
            Pz[k % SLOTS, :, :, :, pl.ds(pl.multiple_of(n * 256, 256), 256)] = block(k, n)
            return carry

        lax.fori_loop(0, ZB, one, 0)

    def pick(d, kind):
        if kind == 0:
            return zo, d
        if kind == 1:
            return (zp, 1) if d == 0 else (zm, 0)
        return (zp, 0) if d == 0 else (zm, 1)

    def z_copy(k, d, kind, cols=slice(0, MC)):
        s = k % SLOTS
        a, b = pick(d, kind)
        return remote(
            Pz.at[s, a, b, :, cols],
            ZR.at[k, d, kind, :, cols],
            zsnd.at[s, 2 * kind + d],
            zrcv.at[k, d, kind],
            up if d == 0 else down,
        )

    late = slice(ZC, MC)

    def y_copy(k):
        s = k % SLOTS
        return remote(Pz.at[s, z, 1 - yl, :, 0:ZC], YR.at[k], zsnd.at[s, 6], yrcv.at[k], ylo)

    def y1_copy(k):
        s = k % SLOTS
        return remote(Py.at[s, 1 - yl], YZ.at[k], zsnd.at[s, 7], y1rcv.at[k], ylo)

    def out_copy(k):
        return pltpu.make_async_copy(OS.at[k], out.at[pl.ds(pl.multiple_of(k * RW, RW), RW)], osem.at[k])

    def add_y1(k):
        y1_copy(k).wait_recv()
        Pz[(k + 1) % SLOTS, :, :, :, late] = Py[k % SLOTS, yl] + YZ[k]

    def z_first(k, cols):
        for kind in range(2):
            for d in range(2):
                z_copy(k, d, kind, cols).start()

    def z_relay(k, cols):
        s = k % SLOTS
        for d in range(2):
            z_copy(k, d, 0, cols).wait_recv()
            a, b = pick(d, 2)
            Pz[s, a, b, :, cols] = Pz[s, a, b, :, cols] + ZR[k, d, 0, :, cols]
            z_copy(k, d, 2, cols).start()

    def z_wait(k, cols):
        for kind in (1, 2):
            for d in range(2):
                z_copy(k, d, kind, cols).wait_recv()

    def z_sum(k, b, cols):
        one, two = (2, 1) if b == 0 else (1, 2)
        return Pz[k % SLOTS, z, b, :, cols] + ZR[k, 0, one, :, cols] + ZR[k, 1, two, :, cols]

    def store_late(k):
        for b in range(2):
            OS[k - 1, :, ZC + 256 * b : ZC + 256 * (b + 1)] = z_sum(k, b, late)

    def z_last(k):
        z_wait(k, slice(0, MC))
        for b in range(2):
            Pz[k % SLOTS, z, b, :, 0:ZC] = z_sum(k, b, slice(0, ZC))
        y_copy(k).start()

        @pl.when(k >= 1)
        def _():
            store_late(k)

    def finish(k):
        s = k % SLOTS
        y_copy(k).wait_recv()
        OS[k, :, 0:ZC] = Pz[s, z, yl, :, 0:ZC] + YR[k]
        out_copy(k).start()

    def free(k):
        for kind in range(3):
            for d in range(2):
                z_copy(k, d, kind).wait_send()
        y_copy(k).wait_send()
        y1_copy(k).wait_send()

    Pz[0, :, :, :, late] = jnp.zeros((4, 2, RW, MC - ZC), F32)

    def step(k, carry):

        @pl.when(k < PH)
        def _():
            wait_rest(k)

        @pl.when((k >= SLOTS) & (k <= PH))
        def _():
            free(k - SLOTS)

        @pl.when(k < PH)
        def _():
            compute_y(k)
            y1_copy(k).start()
            compute_z(k)

        @pl.when((k >= 1) & (k <= PH))
        def _():
            add_y1(k - 1)

        @pl.when(k < PH)
        def _():
            z_first(k, slice(0, MC))

        @pl.when(k == PH)
        def _():
            z_first(k, late)

        @pl.when((k >= 1) & (k <= PH))
        def _():
            z_relay(k - 1, slice(0, MC))

        @pl.when(k == PH + 1)
        def _():
            z_relay(PH, late)

        @pl.when(k == 0)
        def _():
            start_fwd_x(1)
            start_peer_x(2)

        @pl.when(k + 4 < PH)
        def _():
            own_y(k + 4).start()

        @pl.when(k + 3 < PH)
        def _():
            start_own_x(k + 3)

        @pl.when(k + 2 < PH)
        def _():
            start_fwd_x(k + 2)

        @pl.when(k + 3 < PH)
        def _():
            start_peer_x(k + 3)

        @pl.when((k >= 2) & (k <= PH + 1))
        def _():
            z_last(k - 2)

        @pl.when(k == PH + 2)
        def _():
            z_wait(PH, late)
            store_late(PH)

        @pl.when(k >= 3)
        def _():
            finish(k - 3)

        return carry

    lax.fori_loop(0, PH + 3, step, 0)

    def drain(k, carry):
        own_y(k).wait_send()
        for d in range(2):
            own_x(k, d).wait_send()
            peer_x(k, d).wait_send()
            fwd_x(k, d).wait_send()
        return carry

    lax.fori_loop(0, PH, drain, 0)
    lax.fori_loop(PH - SLOTS + 1, PH, lambda k, carry: (free(k), carry)[1], 0)
    for kind in range(3):
        for d in range(2):
            z_copy(PH, d, kind, late).wait_send()
    lax.fori_loop(0, PH, lambda k, carry: (out_copy(k).wait(), carry)[1], 0)


def per_device(activations, out_grads, noise):
    dma = pltpu.SemaphoreType.DMA
    summed = pl.pallas_call(
        kernel,
        out_shape=jax.ShapeDtypeStruct((256, FL), F32),
        in_specs=[pl.BlockSpec(memory_space=pl.ANY)] * 2,
        out_specs=pl.BlockSpec(memory_space=pl.ANY),
        scratch_shapes=[
            pltpu.VMEM((2, TOK, FL), BF16),
            pltpu.VMEM((TOK, DL), BF16),
            pltpu.VMEM((2, PH, RW, TOK), BF16),
            pltpu.VMEM((PH, 8, 2, RW, TOK), BF16),
            pltpu.VMEM((4, 2, GROWS, LANES), F32),
            pltpu.VMEM((2, 4, GROWS, LANES), F32),
            pltpu.VMEM((4, 2, GROWS, LANES), F32),
            pltpu.VMEM((2, GROWS, LANES), F32),
            pltpu.VMEM((GROWS, LANES), F32),
            pltpu.VMEM((4, GROWS, LANES), F32),
            pltpu.VMEM((4, GROWS, LANES), F32),
            pltpu.VMEM((4, GROWS, LANES), F32),
            pltpu.VMEM((8, LANES), F32),
            pltpu.VMEM((8, 8, LANES), F32),
            pltpu.VMEM((2, 8, 256), F32),
            pltpu.VMEM((SLOTS, 4, 2, RW, MC), F32),
            pltpu.VMEM((SLOTS, 2, 4, 2, RW, 256), F32),
            pltpu.VMEM((PH + 1, 2, 3, RW, MC), F32),
            pltpu.VMEM((PH, RW, ZC), F32),
            pltpu.VMEM((PH, 4, 2, RW, 256), F32),
            pltpu.VMEM((PH, RW, FL), F32),
            dma((EX,)),
            dma,
            dma((2,)),
            dma((2,)),
            dma,
            dma((8,)),
            dma((8,)),
            dma((8,)),
            dma((8,)),
            dma((2,)),
            dma((PH, 7)),
            dma((PH, 2, 3)),
            dma((PH,)),
            dma((SLOTS, 8)),
            dma((PH + 1, 2, 3)),
            dma((PH,)),
            dma((PH,)),
            dma((PH,)),
        ],
        compiler_params=pltpu.CompilerParams(
            collective_id=0, has_side_effects=True, vmem_limit_bytes=62 << 20
        ),
        cost_estimate=pl.CostEstimate(flops=24 * 10**9, bytes_accessed=9 * 10**6, transcendentals=0),
    )(activations, out_grads)
    return (summed + noise) / COUNT


def solution(mesh):
    return jax.shard_map(
        per_device,
        mesh=mesh,
        in_specs=(P("dp", "tensor"), P("dp", "tensor"), P("dp", "tensor")),
        out_specs=P("dp", "tensor"),
        check_vma=False,
    )
```

```python
import functools

import jax
import jax.numpy as jnp
from jax import lax
from jax.experimental import pallas as pl
from jax.experimental.pallas import tpu as pltpu
from jax.sharding import PartitionSpec as P

MESH = pl.DeviceIdType.MESH
F32 = jnp.float32
BF16 = jnp.bfloat16
D = 4096
FF = 14336
SEQ = 256
EX = 6
TOK = EX * SEQ
FL = 1792
DL = 512
PH = 16
RW = 16
SLOTS = 4
ZB = 5
ZC = ZB * 256
MC = ZC + 256
GROWS = EX * 32 + 8
COUNT = 96
LANES = 128


def kernel(
    act, g, out,
    H, gin, gT, Gb, GSA, GSG, RA1, A2, RA2, RG1, G2, RG2, SQm, SQ, FAC, Pz, Py, ZR, YR, YZ, OS,
    hsem, gsem, hx, gx, gl, gramS, gramR, sqS, sqR, facx, gsnd, grcv, gy, zsnd, zrcv, yrcv, y1rcv, osem,
):
    dp = lax.axis_index("dp")
    t = lax.axis_index("tensor")
    z, yl, c = dp // 4, (dp // 2) % 2, dp % 2
    x, yh = t // 2, t % 2
    oc = 1 - c
    sib = (z * 4 + yl * 2 + oc, t)
    xp, xm = (x + 1) % 4, (x + 3) % 4
    right = (dp, xp * 2 + yh)
    left = (dp, xm * 2 + yh)
    ypeer = (dp, x * 2 + 1 - yh)
    zp, zm, zo = (z + 1) % 4, (z + 3) % 4, (z + 2) % 4
    up = (zp * 4 + yl * 2 + c, t)
    down = (zm * 4 + yl * 2 + c, t)
    ylo = (z * 4 + (1 - yl) * 2 + c, t)

    def remote(src, dst, ssem, rsem, dev):
        return pltpu.make_async_remote_copy(
            src_ref=src, dst_ref=dst, send_sem=ssem, recv_sem=rsem, device_id=dev, device_id_type=MESH
        )

    g_in = pltpu.make_async_copy(g, gin, gsem)
    g_in.start()

    def h_in(e):
        rows = pl.ds(e * SEQ, SEQ)
        return pltpu.make_async_copy(act.at[rows], H.at[c, rows], hsem.at[e])

    for e in range(EX):
        h_in(e).start()

    barrier = pltpu.get_barrier_semaphore()
    partners = [(dp, (t + j) % 8) for j in range(1, 8)] + [sib, up, down, ylo]
    for dev in partners:
        pl.semaphore_signal(barrier, inc=1, device_id=dev, device_id_type=MESH)

    def shard_copy(k, owner, ssem, rsem, dev):
        part = Gb.at[k, owner]
        return remote(part, part, ssem, rsem, dev)

    def own_y(k):
        return shard_copy(k, t, gsnd.at[k, 0], gy.at[k], ypeer)

    def own_x(k, d):
        return shard_copy(k, t, gsnd.at[k, 1 + d], grcv.at[k, d, 0], right if d == 0 else left)

    def peer_x(k, d):
        return shard_copy(k, x * 2 + 1 - yh, gsnd.at[k, 3 + d], grcv.at[k, d, 1], right if d == 0 else left)

    def fwd_x(k, d):
        owner = xm * 2 if d == 0 else xp * 2 + 1
        return shard_copy(k, owner, gsnd.at[k, 5 + d], grcv.at[k, d, 2], right if d == 0 else left)

    def wait_shard(k, d, kind):
        shard_copy(k, t, gsnd.at[k, 0], grcv.at[k, d, kind], ypeer).wait_recv()

    def start_own_x(k):
        own_x(k, 0).start()
        own_x(k, 1).start()

    def start_peer_x(k):
        own_y(k).wait_recv()
        peer_x(k, 0).start()
        peer_x(k, 1).start()

    def start_fwd_x(k):
        wait_shard(k, 0, yh)
        fwd_x(k, 0).start()
        wait_shard(k, 1, 1 - yh)
        fwd_x(k, 1).start()

    def wait_rest(k):
        wait_shard(k, 0, 1 - yh)
        wait_shard(k, 1, yh)
        wait_shard(k, 0, 2)
        wait_shard(k, 1, 2)

    i0 = lax.broadcasted_iota(jnp.int32, (LANES, LANES), 0)
    i1 = lax.broadcasted_iota(jnp.int32, (LANES, LANES), 1)
    e8 = lax.broadcasted_iota(jnp.int32, (8, LANES), 0)
    nt = (((1,), (1,)), ((), ()))
    zero8 = jnp.zeros((8, LANES), F32)

    def gram(rows_of, piece):
        def one(e, diags):
            r = rows_of(e, pl.ds(pl.multiple_of(e * SEQ, SEQ), SEQ))
            a = lax.dot_general(r, r, nt, preferred_element_type=F32)
            packed = jnp.where(i0 >= i1, a[:LANES, :LANES], a[LANES:, LANES:])
            below = a[LANES:, :LANES]
            for owner in range(8):
                part = packed if owner < 4 else below
                lo = (owner % 4) * 32
                piece(owner, pl.ds(pl.multiple_of(e * 32, 32), 32), part[lo : lo + 32])
            diag = jnp.sum(jnp.where(i0 == i1, a[LANES:, LANES:], 0.0), axis=0, keepdims=True)
            return jnp.where(e8 == e, diag, diags)

        diags = lax.fori_loop(0, EX, one, zero8)
        for owner in range(8):
            piece(owner, slice(EX * 32, GROWS), diags)

    def piece_a(owner, rows, value):
        GSA[owner // 2, owner % 2, rows, :] = value

    def piece_g(owner, rows, value):
        GSG[owner % 2, owner // 2, rows, :] = value

    def rows_h(e, rows):
        h_in(e).wait()
        return H[c, rows, :]

    g_in.wait()
    for e in range(EX):
        tr = gin[e * SEQ : (e + 1) * SEQ, :].T
        gT[:, :, :, e * SEQ : (e + 1) * SEQ] = tr.reshape(2, PH, RW, SEQ)
    g_local = pltpu.make_async_copy(gT.at[c], Gb.at[:, t, c], gl)
    g_local.start()
    pl.semaphore_wait(barrier, len(partners))
    g_sib = remote(gT.at[oc], Gb.at[:, t, c], gx.at[0], gx.at[1], sib)
    g_sib.start()
    gram(lambda e, rows: gin[rows, :], piece_g)
    g_one = remote(GSG.at[1 - yh], RG1, gramS.at[0], gramR.at[0], ypeer)
    g_one.start()
    g_local.wait()
    g_sib.wait()
    own_y(0).start()
    start_own_x(0)
    gram(rows_h, piece_a)

    def x_dev(j):
        return (dp, ((x + j) % 4) * 2 + yh)

    def a_one(j):
        return remote(GSA.at[(x + j) % 4], RA1.at[x], gramS.at[j], gramR.at[j], x_dev(j))

    def g_two(j):
        return remote(G2.at[(x + j) % 4], RG2.at[x], gramS.at[3 + j], gramR.at[3 + j], x_dev(j))

    for j in (2, 1, 3):
        a_one(j).start()
    h_sib = remote(H.at[c], H.at[c], hx.at[0], hx.at[1], sib)
    h_sib.start()

    g_one.wait_recv()
    G2[...] = GSG[yh] + RG1[...]
    for j in (2, 1, 3):
        g_two(j).start()
    start_peer_x(0)
    for j in range(1, 4):
        a_one(j).wait_recv()
    RA1[x] = GSA[x]
    A2[...] = (RA1[0] + RA1[1]) + (RA1[2] + RA1[3])
    a_two = remote(A2.at[1 - yh], RA2, gramS.at[7], gramR.at[7], ypeer)
    a_two.start()
    start_own_x(1)
    for j in range(1, 4):
        g_two(j).wait_recv()
    RG2[x] = G2[x]
    grad_gram = (RG2[0] + RG2[1]) + (RG2[2] + RG2[3])
    a_two.wait_recv()
    prod = (A2[yh] + RA2[...]) * grad_gram

    r32 = lax.broadcasted_iota(jnp.int32, (32, LANES), 0)
    l32 = lax.broadcasted_iota(jnp.int32, (32, LANES), 1)
    weight = jnp.where(l32 == r32 + t * 32, 1.0, 2.0)
    l8 = lax.broadcasted_iota(jnp.int32, (8, LANES), 1)
    mine = jnp.where(l8 // 16 == t, prod[EX * 32 :], 0.0)
    for e in range(EX):
        part = jnp.sum(prod[e * 32 : (e + 1) * 32] * weight, axis=0, keepdims=True)
        mine = mine + jnp.where(e8 == e, part, 0.0)
    SQm[...] = mine
    SQ[t] = mine

    def sq_copy(j):
        peer = (t + j) % 8
        return remote(SQm, SQ.at[t], sqS.at[j], sqR.at[j], (dp, peer))

    for j in range(1, 8):
        sq_copy(j).start()
    start_fwd_x(0)
    for k in range(1, 5):
        own_y(k).start()
    for j in range(1, 8):
        sq_copy(j).wait_recv()
    sq = SQ[0]
    for s in range(1, 8):
        sq = sq + SQ[s]
    sq = jnp.sum(sq, axis=1, keepdims=True)
    bound = jnp.float32(0.15) * jnp.sqrt(jnp.float32(SEQ) * FF * D)
    factor = jnp.minimum(1.0, bound / jnp.sqrt(jnp.maximum(sq, 0.0) + 1e-06))
    FAC[c] = jnp.broadcast_to(factor, (8, 256))
    fac_sib = remote(FAC.at[c], FAC.at[c], facx.at[0], facx.at[1], sib)
    fac_sib.start()
    start_peer_x(1)
    start_own_x(2)
    for k in (5, 6):
        own_y(k).start()
    h_sib.wait()
    fac_sib.wait()
    g_one.wait_send()
    a_two.wait_send()
    for j in range(1, 4):
        a_one(j).wait_send()
        g_two(j).wait_send()
    for j in range(1, 8):
        sq_copy(j).wait_send()

    def block(k, n):
        cols = pl.ds(pl.multiple_of(n * 256, 256), 256)
        acc = None
        for e in range(2 * EX):
            cs, j = divmod(e, EX)
            lhs = Gb[k, :, cs, :, j * SEQ : (j + 1) * SEQ].reshape(8 * RW, SEQ)
            rhs = H[cs, j * SEQ : (j + 1) * SEQ, cols]
            d = jnp.dot(lhs, rhs, preferred_element_type=F32) * FAC[cs, j : j + 1, :]
            acc = d if acc is None else acc + d
        return acc.reshape(4, 2, RW, 256)

    def compute_y(k):
        def one(n, carry):
            r = block(k, n + ZB)
            for b in range(2):
                Py[k % SLOTS, b, :, n] = r[:, b]
            return carry

        lax.fori_loop(0, 2, one, 0)

    def compute_z(k):
        def one(n, carry):
            Pz[k % SLOTS, :, :, :, pl.ds(pl.multiple_of(n * 256, 256), 256)] = block(k, n)
            return carry

        lax.fori_loop(0, ZB, one, 0)

    def pick(d, kind):
        if kind == 0:
            return zo, d
        if kind == 1:
            return (zp, 1) if d == 0 else (zm, 0)
        return (zp, 0) if d == 0 else (zm, 1)

    def z_copy(k, d, kind, cols=slice(0, MC)):
        s = k % SLOTS
        a, b = pick(d, kind)
        return remote(
            Pz.at[s, a, b, :, cols],
            ZR.at[k, d, kind, :, cols],
            zsnd.at[s, 2 * kind + d],
            zrcv.at[k, d, kind],
            up if d == 0 else down,
        )

    late = slice(ZC, MC)

    def y_copy(k):
        s = k % SLOTS
        return remote(Pz.at[s, z, 1 - yl, :, 0:ZC], YR.at[k], zsnd.at[s, 6], yrcv.at[k], ylo)

    def y1_copy(k):
        s = k % SLOTS
        return remote(Py.at[s, 1 - yl], YZ.at[k], zsnd.at[s, 7], y1rcv.at[k], ylo)

    def out_copy(k):
        return pltpu.make_async_copy(OS.at[k], out.at[pl.ds(pl.multiple_of(k * RW, RW), RW)], osem.at[k])

    def add_y1(k):
        y1_copy(k).wait_recv()
        Pz[(k + 1) % SLOTS, :, :, :, late] = Py[k % SLOTS, yl] + YZ[k]

    def z_first(k, cols):
        for kind in range(2):
            for d in range(2):
                z_copy(k, d, kind, cols).start()

    def z_relay(k, cols):
        s = k % SLOTS
        for d in range(2):
            z_copy(k, d, 0, cols).wait_recv()
            a, b = pick(d, 2)
            Pz[s, a, b, :, cols] = Pz[s, a, b, :, cols] + ZR[k, d, 0, :, cols]
            z_copy(k, d, 2, cols).start()

    def z_wait(k, cols):
        for kind in (1, 2):
            for d in range(2):
                z_copy(k, d, kind, cols).wait_recv()

    def z_sum(k, b, cols):
        one, two = (2, 1) if b == 0 else (1, 2)
        return Pz[k % SLOTS, z, b, :, cols] + ZR[k, 0, one, :, cols] + ZR[k, 1, two, :, cols]

    def store_late(k):
        for b in range(2):
            OS[k - 1, :, ZC + 256 * b : ZC + 256 * (b + 1)] = z_sum(k, b, late)

    def z_last(k):
        z_wait(k, slice(0, MC))
        for b in range(2):
            Pz[k % SLOTS, z, b, :, 0:ZC] = z_sum(k, b, slice(0, ZC))
        y_copy(k).start()

        @pl.when(k >= 1)
        def _():
            store_late(k)

    def finish(k):
        s = k % SLOTS
        y_copy(k).wait_recv()
        OS[k, :, 0:ZC] = Pz[s, z, yl, :, 0:ZC] + YR[k]
        out_copy(k).start()

    def free(k):
        for kind in range(3):
            for d in range(2):
                z_copy(k, d, kind).wait_send()
        y_copy(k).wait_send()
        y1_copy(k).wait_send()

    Pz[0, :, :, :, late] = jnp.zeros((4, 2, RW, MC - ZC), F32)

    def step(k, carry):

        @pl.when(k < PH)
        def _():
            wait_rest(k)

        @pl.when((k >= SLOTS) & (k <= PH))
        def _():
            free(k - SLOTS)

        @pl.when(k < PH)
        def _():
            compute_y(k)
            y1_copy(k).start()
            compute_z(k)

        @pl.when((k >= 1) & (k <= PH))
        def _():
            add_y1(k - 1)

        @pl.when(k < PH)
        def _():
            z_first(k, slice(0, MC))

        @pl.when(k == PH)
        def _():
            z_first(k, late)

        @pl.when((k >= 1) & (k <= PH))
        def _():
            z_relay(k - 1, slice(0, MC))

        @pl.when(k == PH + 1)
        def _():
            z_relay(PH, late)

        @pl.when(k == 0)
        def _():
            start_fwd_x(1)
            start_peer_x(2)

        @pl.when(k + 7 < PH)
        def _():
            own_y(k + 7).start()

        @pl.when(k + 3 < PH)
        def _():
            start_own_x(k + 3)

        @pl.when(k + 3 < PH)
        def _():
            start_peer_x(k + 3)

        @pl.when(k + 2 < PH)
        def _():
            start_fwd_x(k + 2)

        @pl.when((k >= 2) & (k <= PH + 1))
        def _():
            z_last(k - 2)

        @pl.when(k == PH + 2)
        def _():
            z_wait(PH, late)
            store_late(PH)

        @pl.when(k >= 3)
        def _():
            finish(k - 3)

        return carry

    lax.fori_loop(0, PH + 3, step, 0)

    def drain(k, carry):
        own_y(k).wait_send()
        for d in range(2):
            own_x(k, d).wait_send()
            peer_x(k, d).wait_send()
            fwd_x(k, d).wait_send()
        return carry

    lax.fori_loop(0, PH, drain, 0)
    lax.fori_loop(PH - SLOTS + 1, PH, lambda k, carry: (free(k), carry)[1], 0)
    for kind in range(3):
        for d in range(2):
            z_copy(PH, d, kind, late).wait_send()
    lax.fori_loop(0, PH, lambda k, carry: (out_copy(k).wait(), carry)[1], 0)


def per_device(activations, out_grads, noise):
    dma = pltpu.SemaphoreType.DMA
    summed = pl.pallas_call(
        kernel,
        out_shape=jax.ShapeDtypeStruct((256, FL), F32),
        in_specs=[pl.BlockSpec(memory_space=pl.ANY)] * 2,
        out_specs=pl.BlockSpec(memory_space=pl.ANY),
        scratch_shapes=[
            pltpu.VMEM((2, TOK, FL), BF16),
            pltpu.VMEM((TOK, DL), BF16),
            pltpu.VMEM((2, PH, RW, TOK), BF16),
            pltpu.VMEM((PH, 8, 2, RW, TOK), BF16),
            pltpu.VMEM((4, 2, GROWS, LANES), F32),
            pltpu.VMEM((2, 4, GROWS, LANES), F32),
            pltpu.VMEM((4, 2, GROWS, LANES), F32),
            pltpu.VMEM((2, GROWS, LANES), F32),
            pltpu.VMEM((GROWS, LANES), F32),
            pltpu.VMEM((4, GROWS, LANES), F32),
            pltpu.VMEM((4, GROWS, LANES), F32),
            pltpu.VMEM((4, GROWS, LANES), F32),
            pltpu.VMEM((8, LANES), F32),
            pltpu.VMEM((8, 8, LANES), F32),
            pltpu.VMEM((2, 8, 256), F32),
            pltpu.VMEM((SLOTS, 4, 2, RW, MC), F32),
            pltpu.VMEM((SLOTS, 2, 4, 2, RW, 256), F32),
            pltpu.VMEM((PH + 1, 2, 3, RW, MC), F32),
            pltpu.VMEM((PH, RW, ZC), F32),
            pltpu.VMEM((PH, 4, 2, RW, 256), F32),
            pltpu.VMEM((PH, RW, FL), F32),
            dma((EX,)),
            dma,
            dma((2,)),
            dma((2,)),
            dma,
            dma((8,)),
            dma((8,)),
            dma((8,)),
            dma((8,)),
            dma((2,)),
            dma((PH, 7)),
            dma((PH, 2, 3)),
            dma((PH,)),
            dma((SLOTS, 8)),
            dma((PH + 1, 2, 3)),
            dma((PH,)),
            dma((PH,)),
            dma((PH,)),
        ],
        compiler_params=pltpu.CompilerParams(
            collective_id=0, has_side_effects=True, vmem_limit_bytes=62 << 20
        ),
        cost_estimate=pl.CostEstimate(flops=24 * 10**9, bytes_accessed=9 * 10**6, transcendentals=0),
    )(activations, out_grads)
    return (summed + noise) / COUNT


def solution(mesh):
    return jax.shard_map(
        per_device,
        mesh=mesh,
        in_specs=(P("dp", "tensor"), P("dp", "tensor"), P("dp", "tensor")),
        out_specs=P("dp", "tensor"),
        check_vma=False,
    )
```

```python
import functools

import jax
import jax.numpy as jnp
from jax import lax
from jax.experimental import pallas as pl
from jax.experimental.pallas import tpu as pltpu
from jax.sharding import PartitionSpec as P

MESH = pl.DeviceIdType.MESH
F32 = jnp.float32
BF16 = jnp.bfloat16
D = 4096
FF = 14336
SEQ = 256
EX = 6
TOK = EX * SEQ
FL = 1792
DL = 512
PH = 16
RW = 16
SLOTS = 4
ZB = 5
ZC = ZB * 256
MC = ZC + 256
GROWS = EX * 32 + 8
COUNT = 96
LANES = 128


def kernel(
    act, g, out,
    H, gin, gT, Gb, GSA, GSG, RA1, A2, RA2, RG1, G2, RG2, SQm, SQ, FAC, Pz, Py, ZR, YR, YZ, OS,
    hsem, gsem, hx, gx, gl, gramS, gramR, sqS, sqR, facx, gsnd, grcv, gy, zsnd, zrcv, yrcv, y1rcv, osem,
):
    dp = lax.axis_index("dp")
    t = lax.axis_index("tensor")
    z, yl, c = dp // 4, (dp // 2) % 2, dp % 2
    x, yh = t // 2, t % 2
    oc = 1 - c
    sib = (z * 4 + yl * 2 + oc, t)
    xp, xm = (x + 1) % 4, (x + 3) % 4
    right = (dp, xp * 2 + yh)
    left = (dp, xm * 2 + yh)
    ypeer = (dp, x * 2 + 1 - yh)
    zp, zm, zo = (z + 1) % 4, (z + 3) % 4, (z + 2) % 4
    up = (zp * 4 + yl * 2 + c, t)
    down = (zm * 4 + yl * 2 + c, t)
    ylo = (z * 4 + (1 - yl) * 2 + c, t)

    def remote(src, dst, ssem, rsem, dev):
        return pltpu.make_async_remote_copy(
            src_ref=src, dst_ref=dst, send_sem=ssem, recv_sem=rsem, device_id=dev, device_id_type=MESH
        )

    g_in = pltpu.make_async_copy(g, gin, gsem)
    g_in.start()

    def h_in(e):
        rows = pl.ds(e * SEQ, SEQ)
        return pltpu.make_async_copy(act.at[rows], H.at[c, rows], hsem.at[e])

    for e in range(EX):
        h_in(e).start()

    barrier = pltpu.get_barrier_semaphore()
    partners = [(dp, (t + j) % 8) for j in range(1, 8)] + [sib, up, down, ylo]
    for dev in partners:
        pl.semaphore_signal(barrier, inc=1, device_id=dev, device_id_type=MESH)

    def shard_copy(k, owner, ssem, rsem, dev):
        part = Gb.at[k, owner]
        return remote(part, part, ssem, rsem, dev)

    def own_y(k):
        return shard_copy(k, t, gsnd.at[k, 0], gy.at[k], ypeer)

    def own_x(k, d):
        return shard_copy(k, t, gsnd.at[k, 1 + d], grcv.at[k, d, 0], right if d == 0 else left)

    def peer_x(k, d):
        return shard_copy(k, x * 2 + 1 - yh, gsnd.at[k, 3 + d], grcv.at[k, d, 1], right if d == 0 else left)

    def fwd_x(k, d):
        owner = xm * 2 if d == 0 else xp * 2 + 1
        return shard_copy(k, owner, gsnd.at[k, 5 + d], grcv.at[k, d, 2], right if d == 0 else left)

    def wait_shard(k, d, kind):
        shard_copy(k, t, gsnd.at[k, 0], grcv.at[k, d, kind], ypeer).wait_recv()

    def start_own_x(k):
        own_x(k, 0).start()
        own_x(k, 1).start()

    def start_peer_x(k):
        own_y(k).wait_recv()
        peer_x(k, 0).start()
        peer_x(k, 1).start()

    def start_fwd_x(k):
        wait_shard(k, 0, yh)
        fwd_x(k, 0).start()
        wait_shard(k, 1, 1 - yh)
        fwd_x(k, 1).start()

    def wait_rest(k):
        wait_shard(k, 0, 1 - yh)
        wait_shard(k, 1, yh)
        wait_shard(k, 0, 2)
        wait_shard(k, 1, 2)

    i0 = lax.broadcasted_iota(jnp.int32, (LANES, LANES), 0)
    i1 = lax.broadcasted_iota(jnp.int32, (LANES, LANES), 1)
    e8 = lax.broadcasted_iota(jnp.int32, (8, LANES), 0)
    nt = (((1,), (1,)), ((), ()))
    zero8 = jnp.zeros((8, LANES), F32)

    def gram(rows_of, piece):
        def one(e, diags):
            r = rows_of(e, pl.ds(pl.multiple_of(e * SEQ, SEQ), SEQ))
            a = lax.dot_general(r, r, nt, preferred_element_type=F32)
            packed = jnp.where(i0 >= i1, a[:LANES, :LANES], a[LANES:, LANES:])
            below = a[LANES:, :LANES]
            for owner in range(8):
                part = packed if owner < 4 else below
                lo = (owner % 4) * 32
                piece(owner, pl.ds(pl.multiple_of(e * 32, 32), 32), part[lo : lo + 32])
            diag = jnp.sum(jnp.where(i0 == i1, a[LANES:, LANES:], 0.0), axis=0, keepdims=True)
            return jnp.where(e8 == e, diag, diags)

        diags = lax.fori_loop(0, EX, one, zero8)
        for owner in range(8):
            piece(owner, slice(EX * 32, GROWS), diags)

    def piece_a(owner, rows, value):
        GSA[owner // 2, owner % 2, rows, :] = value

    def piece_g(owner, rows, value):
        GSG[owner % 2, owner // 2, rows, :] = value

    def rows_h(e, rows):
        h_in(e).wait()
        return H[c, rows, :]

    g_in.wait()
    for e in range(EX):
        tr = gin[e * SEQ : (e + 1) * SEQ, :].T
        gT[:, :, :, e * SEQ : (e + 1) * SEQ] = tr.reshape(2, PH, RW, SEQ)
    g_local = pltpu.make_async_copy(gT.at[c], Gb.at[:, t, c], gl)
    g_local.start()
    pl.semaphore_wait(barrier, len(partners))
    g_sib = remote(gT.at[oc], Gb.at[:, t, c], gx.at[0], gx.at[1], sib)
    g_sib.start()
    gram(lambda e, rows: gin[rows, :], piece_g)
    g_one = remote(GSG.at[1 - yh], RG1, gramS.at[0], gramR.at[0], ypeer)
    g_one.start()
    g_local.wait()
    g_sib.wait()
    own_y(0).start()
    start_own_x(0)
    gram(rows_h, piece_a)

    def x_dev(j):
        return (dp, ((x + j) % 4) * 2 + yh)

    def a_one(j):
        return remote(GSA.at[(x + j) % 4], RA1.at[x], gramS.at[j], gramR.at[j], x_dev(j))

    def g_two(j):
        return remote(G2.at[(x + j) % 4], RG2.at[x], gramS.at[3 + j], gramR.at[3 + j], x_dev(j))

    for j in (2, 1, 3):
        a_one(j).start()
    h_sib = remote(H.at[c], H.at[c], hx.at[0], hx.at[1], sib)
    h_sib.start()

    g_one.wait_recv()
    G2[...] = GSG[yh] + RG1[...]
    for j in (2, 1, 3):
        g_two(j).start()
    start_peer_x(0)
    for j in range(1, 4):
        a_one(j).wait_recv()
    RA1[x] = GSA[x]
    A2[...] = (RA1[0] + RA1[1]) + (RA1[2] + RA1[3])
    a_two = remote(A2.at[1 - yh], RA2, gramS.at[7], gramR.at[7], ypeer)
    a_two.start()
    start_own_x(1)
    for j in range(1, 4):
        g_two(j).wait_recv()
    RG2[x] = G2[x]
    grad_gram = (RG2[0] + RG2[1]) + (RG2[2] + RG2[3])
    a_two.wait_recv()
    prod = (A2[yh] + RA2[...]) * grad_gram

    r32 = lax.broadcasted_iota(jnp.int32, (32, LANES), 0)
    l32 = lax.broadcasted_iota(jnp.int32, (32, LANES), 1)
    weight = jnp.where(l32 == r32 + t * 32, 1.0, 2.0)
    l8 = lax.broadcasted_iota(jnp.int32, (8, LANES), 1)
    mine = jnp.where(l8 // 16 == t, prod[EX * 32 :], 0.0)
    for e in range(EX):
        part = jnp.sum(prod[e * 32 : (e + 1) * 32] * weight, axis=0, keepdims=True)
        mine = mine + jnp.where(e8 == e, part, 0.0)
    SQm[...] = mine
    SQ[t] = mine

    def sq_copy(j):
        peer = (t + j) % 8
        return remote(SQm, SQ.at[t], sqS.at[j], sqR.at[j], (dp, peer))

    for j in range(1, 8):
        sq_copy(j).start()
    start_fwd_x(0)
    for k in range(1, 5):
        own_y(k).start()
    for j in range(1, 8):
        sq_copy(j).wait_recv()
    sq = SQ[0]
    for s in range(1, 8):
        sq = sq + SQ[s]
    sq = jnp.sum(sq, axis=1, keepdims=True)
    bound = jnp.float32(0.15) * jnp.sqrt(jnp.float32(SEQ) * FF * D)
    factor = jnp.minimum(1.0, bound / jnp.sqrt(jnp.maximum(sq, 0.0) + 1e-06))
    FAC[c] = jnp.broadcast_to(factor, (8, 256))
    fac_sib = remote(FAC.at[c], FAC.at[c], facx.at[0], facx.at[1], sib)
    fac_sib.start()
    start_peer_x(1)
    start_own_x(2)
    for k in (5, 6):
        own_y(k).start()
    h_sib.wait()
    fac_sib.wait()
    g_one.wait_send()
    a_two.wait_send()
    for j in range(1, 4):
        a_one(j).wait_send()
        g_two(j).wait_send()
    for j in range(1, 8):
        sq_copy(j).wait_send()

    def block(k, n):
        cols = pl.ds(pl.multiple_of(n * 256, 256), 256)
        acc = None
        for e in range(2 * EX):
            cs, j = divmod(e, EX)
            lhs = Gb[k, :, cs, :, j * SEQ : (j + 1) * SEQ].reshape(8 * RW, SEQ)
            rhs = H[cs, j * SEQ : (j + 1) * SEQ, cols]
            d = jnp.dot(lhs, rhs, preferred_element_type=F32) * FAC[cs, j : j + 1, :]
            acc = d if acc is None else acc + d
        return acc.reshape(4, 2, RW, 256)

    def compute_y(k):
        def one(n, carry):
            r = block(k, n + ZB)
            for b in range(2):
                Py[k % SLOTS, b, :, n] = r[:, b]
            return carry

        lax.fori_loop(0, 2, one, 0)

    def compute_z(k):
        def one(n, carry):
            Pz[k % SLOTS, :, :, :, pl.ds(pl.multiple_of(n * 256, 256), 256)] = block(k, n)
            return carry

        lax.fori_loop(0, ZB, one, 0)

    def pick(d, kind):
        if kind == 0:
            return zo, d
        if kind == 1:
            return (zp, 1) if d == 0 else (zm, 0)
        return (zp, 0) if d == 0 else (zm, 1)

    def z_copy(k, d, kind, cols=slice(0, MC)):
        s = k % SLOTS
        a, b = pick(d, kind)
        return remote(
            Pz.at[s, a, b, :, cols],
            ZR.at[k, d, kind, :, cols],
            zsnd.at[s, 2 * kind + d],
            zrcv.at[k, d, kind],
            up if d == 0 else down,
        )

    late = slice(ZC, MC)

    def y_copy(k):
        s = k % SLOTS
        return remote(Pz.at[s, z, 1 - yl, :, 0:ZC], YR.at[k], zsnd.at[s, 6], yrcv.at[k], ylo)

    def y1_copy(k):
        s = k % SLOTS
        return remote(Py.at[s, 1 - yl], YZ.at[k], zsnd.at[s, 7], y1rcv.at[k], ylo)

    def out_copy(k):
        return pltpu.make_async_copy(OS.at[k], out.at[pl.ds(pl.multiple_of(k * RW, RW), RW)], osem.at[k])

    def add_y1(k):
        y1_copy(k).wait_recv()
        Pz[(k + 1) % SLOTS, :, :, :, late] = Py[k % SLOTS, yl] + YZ[k]

    def z_first(k, cols, kinds=(0, 1)):
        for kind in kinds:
            for d in range(2):
                z_copy(k, d, kind, cols).start()

    def z_relay(k, cols):
        s = k % SLOTS
        for d in range(2):
            z_copy(k, d, 0, cols).wait_recv()
            a, b = pick(d, 2)
            Pz[s, a, b, :, cols] = Pz[s, a, b, :, cols] + ZR[k, d, 0, :, cols]
            z_copy(k, d, 2, cols).start()

    def z_wait(k, cols):
        for kind in (1, 2):
            for d in range(2):
                z_copy(k, d, kind, cols).wait_recv()

    def z_sum(k, b, cols):
        one, two = (2, 1) if b == 0 else (1, 2)
        return Pz[k % SLOTS, z, b, :, cols] + ZR[k, 0, one, :, cols] + ZR[k, 1, two, :, cols]

    def store_late(k):
        for b in range(2):
            OS[k - 1, :, ZC + 256 * b : ZC + 256 * (b + 1)] = z_sum(k, b, late)

    def z_last(k):
        z_wait(k, slice(0, MC))
        for b in range(2):
            Pz[k % SLOTS, z, b, :, 0:ZC] = z_sum(k, b, slice(0, ZC))
        y_copy(k).start()

        @pl.when(k >= 1)
        def _():
            store_late(k)

    def finish(k):
        s = k % SLOTS
        y_copy(k).wait_recv()
        OS[k, :, 0:ZC] = Pz[s, z, yl, :, 0:ZC] + YR[k]
        out_copy(k).start()

    def free(k):
        for kind in range(3):
            for d in range(2):
                z_copy(k, d, kind).wait_send()
        y_copy(k).wait_send()
        y1_copy(k).wait_send()

    Pz[0, :, :, :, late] = jnp.zeros((4, 2, RW, MC - ZC), F32)

    def step(k, carry):

        @pl.when(k < PH)
        def _():
            wait_rest(k)

        @pl.when((k >= SLOTS) & (k <= PH))
        def _():
            free(k - SLOTS)

        @pl.when(k < PH)
        def _():
            compute_y(k)
            y1_copy(k).start()
            compute_z(k)

        @pl.when((k >= 1) & (k <= PH))
        def _():
            add_y1(k - 1)

        @pl.when(k < PH)
        def _():
            z_first(k, slice(0, MC), (0,))

        @pl.when(k == PH)
        def _():
            z_first(k, late)

        @pl.when((k >= 1) & (k <= PH))
        def _():
            z_relay(k - 1, slice(0, MC))

        @pl.when(k < PH)
        def _():
            z_first(k, slice(0, MC), (1,))

        @pl.when(k == PH + 1)
        def _():
            z_relay(PH, late)

        @pl.when(k == 0)
        def _():
            start_fwd_x(1)
            start_peer_x(2)

        @pl.when(k + 7 < PH)
        def _():
            own_y(k + 7).start()

        @pl.when(k + 3 < PH)
        def _():
            start_own_x(k + 3)

        @pl.when(k + 3 < PH)
        def _():
            start_peer_x(k + 3)

        @pl.when(k + 2 < PH)
        def _():
            start_fwd_x(k + 2)

        @pl.when((k >= 2) & (k <= PH + 1))
        def _():
            z_last(k - 2)

        @pl.when(k == PH + 2)
        def _():
            z_wait(PH, late)
            store_late(PH)

        @pl.when(k >= 3)
        def _():
            finish(k - 3)

        return carry

    lax.fori_loop(0, PH + 3, step, 0)

    def drain(k, carry):
        own_y(k).wait_send()
        for d in range(2):
            own_x(k, d).wait_send()
            peer_x(k, d).wait_send()
            fwd_x(k, d).wait_send()
        return carry

    lax.fori_loop(0, PH, drain, 0)
    lax.fori_loop(PH - SLOTS + 1, PH, lambda k, carry: (free(k), carry)[1], 0)
    for kind in range(3):
        for d in range(2):
            z_copy(PH, d, kind, late).wait_send()
    lax.fori_loop(0, PH, lambda k, carry: (out_copy(k).wait(), carry)[1], 0)


def per_device(activations, out_grads, noise):
    dma = pltpu.SemaphoreType.DMA
    summed = pl.pallas_call(
        kernel,
        out_shape=jax.ShapeDtypeStruct((256, FL), F32),
        in_specs=[pl.BlockSpec(memory_space=pl.ANY)] * 2,
        out_specs=pl.BlockSpec(memory_space=pl.ANY),
        scratch_shapes=[
            pltpu.VMEM((2, TOK, FL), BF16),
            pltpu.VMEM((TOK, DL), BF16),
            pltpu.VMEM((2, PH, RW, TOK), BF16),
            pltpu.VMEM((PH, 8, 2, RW, TOK), BF16),
            pltpu.VMEM((4, 2, GROWS, LANES), F32),
            pltpu.VMEM((2, 4, GROWS, LANES), F32),
            pltpu.VMEM((4, 2, GROWS, LANES), F32),
            pltpu.VMEM((2, GROWS, LANES), F32),
            pltpu.VMEM((GROWS, LANES), F32),
            pltpu.VMEM((4, GROWS, LANES), F32),
            pltpu.VMEM((4, GROWS, LANES), F32),
            pltpu.VMEM((4, GROWS, LANES), F32),
            pltpu.VMEM((8, LANES), F32),
            pltpu.VMEM((8, 8, LANES), F32),
            pltpu.VMEM((2, 8, 256), F32),
            pltpu.VMEM((SLOTS, 4, 2, RW, MC), F32),
            pltpu.VMEM((SLOTS, 2, 4, 2, RW, 256), F32),
            pltpu.VMEM((PH + 1, 2, 3, RW, MC), F32),
            pltpu.VMEM((PH, RW, ZC), F32),
            pltpu.VMEM((PH, 4, 2, RW, 256), F32),
            pltpu.VMEM((PH, RW, FL), F32),
            dma((EX,)),
            dma,
            dma((2,)),
            dma((2,)),
            dma,
            dma((8,)),
            dma((8,)),
            dma((8,)),
            dma((8,)),
            dma((2,)),
            dma((PH, 7)),
            dma((PH, 2, 3)),
            dma((PH,)),
            dma((SLOTS, 8)),
            dma((PH + 1, 2, 3)),
            dma((PH,)),
            dma((PH,)),
            dma((PH,)),
        ],
        compiler_params=pltpu.CompilerParams(
            collective_id=0, has_side_effects=True, vmem_limit_bytes=62 << 20
        ),
        cost_estimate=pl.CostEstimate(flops=24 * 10**9, bytes_accessed=9 * 10**6, transcendentals=0),
    )(activations, out_grads)
    return (summed + noise) / COUNT


def solution(mesh):
    return jax.shard_map(
        per_device,
        mesh=mesh,
        in_specs=(P("dp", "tensor"), P("dp", "tensor"), P("dp", "tensor")),
        out_specs=P("dp", "tensor"),
        check_vma=False,
    )
```
